32 devices in a mesh: dp: 16 (over z, y, x), tensor: 2 (over core).
Axes of the slice: x: 2, y: 2, z: 4, core: 2. Of those that a mesh axis runs over, the one named last changes fastest.
Arguments:
- tokens: bfloat16 [16384, 768], P(('dp', 'tensor')), may hold values from -6 to 6
- segment_ids: int32 [16384], P(('dp', 'tensor')), may hold values from 0 to 11, as said below
- w_query: bfloat16 [768, 768], P(None, 'tensor'), may hold values from -0.21875 to 0.21875
- w_key: bfloat16 [768, 768], P(None, 'tensor'), may hold values from -0.21875 to 0.21875
- w_value: bfloat16 [768, 768], P(None, 'tensor'), may hold values from -0.21875 to 0.21875
- b_query: float32 [768], P('tensor'), may hold values from -3 to 3
- b_value: float32 [768], P('tensor'), may hold values from -3 to 3
- w_out: bfloat16 [768, 768], P('tensor'), may hold values from -0.625 to 0.625
- b_out: float32 [768], replicated, may hold values from -3 to 3
- gain_attn: float32 [768], replicated, may hold values from 0.5 to 1.5
- shift_attn: float32 [768], replicated, may hold values from -3 to 3
- w_up: bfloat16 [768, 3072], P(None, 'tensor'), may hold values from -0.21875 to 0.21875
- b_up: float32 [3072], P('tensor'), may hold values from -3 to 3
- w_down: bfloat16 [3072, 768], P('tensor'), may hold values from -0.109375 to 0.109375
- b_down: float32 [768], replicated, may hold values from -3 to 3
- gain_ffn: float32 [768], replicated, may hold values from 0.5 to 1.5
- shift_ffn: float32 [768], replicated, may hold values from -2 to 2
- cotangent: bfloat16 [16384, 768], P(('dp', 'tensor')), may hold values from -7.5 to 7.5
Outputs:
- mixed: bfloat16 [16384, 768], P(('dp', 'tensor'))
- grad_tokens: float32 [16384, 768], P(('dp', 'tensor'))
- grad_w_query: float32 [768, 768], P(None, 'tensor')
- grad_w_key: float32 [768, 768], P(None, 'tensor')
- grad_w_value: float32 [768, 768], P(None, 'tensor')
- grad_b_query: float32 [768], P('tensor')
- grad_b_value: float32 [768], P('tensor')
- grad_w_out: float32 [768, 768], P('tensor')
- grad_b_out: float32 [768], replicated
- grad_gain_attn: float32 [768], replicated
- grad_shift_attn: float32 [768], replicated
- grad_w_up: float32 [768, 3072], P(None, 'tensor')
- grad_b_up: float32 [3072], P('tensor')
- grad_w_down: float32 [3072, 768], P('tensor')
- grad_b_down: float32 [768], replicated
- grad_gain_ffn: float32 [768], replicated
- grad_shift_ffn: float32 [768], replicated
The draws below stay inside these ranges and needn't reach their ends.
Inputs may be any that keep to these rules, and one draw needn't show every extreme that they name: `segment_ids`: within each row of 1024 tokens the numbers start at 0 and never fall; equal numbers in one row mark one sentence or the row's trailing padding, which is never empty.
All inputs are finite; a program needn't handle non-finite values.
Results may differ from the reference program's by a relative error of at most 0.014.
Values may be sent and summed in bfloat16 or wider, within the bound.
No kernel may reach another device: no remote copies, remote signals or barrier semaphores. Data moves between devices by JAX's collectives and lax.ppermute only.
A program may use at most 128 MiB of HBM per device.

```python
import jax
import jax.numpy as jnp
from jax import lax

HEADS = 12
HD = 64
FF = 3072
D = 768
LEN = 1024
TOKENS = 16384


def draw_segment_ids(key, part):
    key = jax.random.fold_in(key, 11)
    row_count = TOKENS // LEN
    streams = jax.random.split(key, 5)
    middle = LEN // 2
    opening = jax.random.randint(streams[0], (row_count, 1), LEN // 4, middle - LEN // 16 + 1)
    closing = jax.random.randint(streams[1], (row_count, 1), middle + LEN // 16, 3 * LEN // 4 + 1)
    padding = jax.random.randint(streams[2], (row_count, 1), 7 * LEN // 8, LEN)
    before = jax.random.randint(streams[3], (row_count, 4), 1, opening)
    after = jax.random.randint(streams[4], (row_count, 4), closing + 1, padding)
    cuts = jnp.concatenate([before, opening, closing, after, padding], axis=1)
    places = jnp.arange(LEN, dtype=jnp.int32)
    numbers = jnp.sum((cuts[:, None, :] <= places[None, :, None]).astype(jnp.int32), axis=2)
    return numbers.reshape(TOKENS).astype(jnp.int32)


def draw_cotangent(key, part):
    key = jax.random.fold_in(key, 23)
    first = jax.random.fold_in(key, 0)
    places = jnp.arange(TOKENS, dtype=jnp.float32) / max(TOKENS - 1, 1)
    factor = (0.6 + 1.2 * places)[:, None]
    base = jax.random.truncated_normal(first, -4.0, 4.0, (TOKENS, D), jnp.float32)
    return (base * factor).astype(jnp.bfloat16)


def levels(own_key, shape, pieces, least, high):
    level, own = 1.0, jax.random.fold_in(own_key, 6)
    for position, blocks in pieces:
        heights = jnp.exp(jax.random.uniform(jax.random.fold_in(own, position), (blocks,), jnp.float32, least / len(pieces), high / len(pieces)))
        level = level * jnp.repeat(heights, shape[position] // blocks).reshape([-1 if axis == position else 1 for axis in range(len(shape))])
    return level


def scatter_about(own_key, dims, width, most, cuts=(), held_as=jnp.bfloat16):
    array = jax.random.normal(own_key, dims, jnp.float32) * width
    if len(cuts) > 0:
        array = levels(own_key, dims, cuts, -0.22, 0.18) * array
    return jnp.clip(array, min=-most, max=most).astype(held_as)


def setup_inputs(seed: int = 0) -> dict:
    splits = jax.random.split(jax.random.key(seed), 19)
    tokens = scatter_about(splits[0], (TOKENS, D), 1.0, 6.0, ((0, 32),))
    segment_ids = draw_segment_ids(jax.random.fold_in(splits[18], 71), 0)
    w_query = scatter_about(splits[2], (D, D), D ** -0.5, 0.21875, ((1, 2),))
    w_key = scatter_about(splits[3], (D, D), D ** -0.5, 0.21875, ((1, 2),))
    w_value = scatter_about(splits[4], (D, D), D ** -0.5, 0.21875, ((1, 2),))
    b_query = scatter_about(splits[5], (D,), 0.5, 3.0, ((0, 2),), jnp.float32)
    b_value = scatter_about(splits[6], (D,), 0.5, 3.0, ((0, 2),), jnp.float32)
    w_out = scatter_about(splits[7], (D, D), (D // 8) ** -0.5, 0.625, ((0, 2),))
    b_out = scatter_about(splits[8], (D,), 0.5, 3.0, (), jnp.float32)
    gain_attn = jnp.clip(1.0 + 0.1 * jax.random.normal(splits[9], (D,), jnp.float32), 0.5, 1.5)
    shift_attn = scatter_about(splits[10], (D,), 0.5, 3.0, (), jnp.float32)
    w_up = scatter_about(splits[11], (D, FF), D ** -0.5, 0.21875, ((1, 2),))
    b_up = scatter_about(splits[12], (FF,), 0.5, 3.0, ((0, 2),), jnp.float32)
    w_down = scatter_about(splits[13], (FF, D), FF ** -0.5, 0.109375, ((0, 2),))
    b_down = scatter_about(splits[14], (D,), 0.5, 3.0, (), jnp.float32)
    gain_ffn = jnp.clip(1.0 + 0.1 * jax.random.normal(splits[15], (D,), jnp.float32), 0.5, 1.5)
    shift_ffn = scatter_about(splits[16], (D,), 0.3, 2.0, (), jnp.float32)
    cotangent = draw_cotangent(jax.random.fold_in(splits[18], 71), 0)
    return dict(tokens=tokens, segment_ids=segment_ids, w_query=w_query, w_key=w_key, w_value=w_value, b_query=b_query, b_value=b_value, w_out=w_out, b_out=b_out, gain_attn=gain_attn, shift_attn=shift_attn, w_up=w_up, b_up=b_up, w_down=w_down, b_down=b_down, gain_ffn=gain_ffn, shift_ffn=shift_ffn, cotangent=cotangent)


EPSILON = 1e-05
HIGHEST = lax.Precision.HIGHEST

@jax.custom_vjp
def low(v):
    return lax.optimization_barrier(v.astype(jnp.bfloat16)).astype(jnp.float32)

@jax.custom_vjp
def low_back(v):
    return v

def low_keep(v):
    return (low(v), None)

def low_pass(kept, grad):
    return (grad,)

def back_keep(v):
    return (v, None)

def back_low(kept, grad):
    return (low(grad),)
low.defvjp(low_keep, low_pass)
low_back.defvjp(back_keep, back_low)

def matmul(left, right):
    return jnp.dot(left, right, precision=HIGHEST, preferred_element_type=jnp.float32)

def normalize(hidden, gain, shift):
    average = lax.optimization_barrier(jnp.mean(hidden, axis=-1, keepdims=True))
    centred = hidden - average
    spread = lax.optimization_barrier(jnp.mean(centred * centred, axis=-1, keepdims=True))
    return centred * lax.rsqrt(spread + EPSILON) * gain + shift

def encoder(inputs, segments, w_query, w_key, w_value, b_query, b_value, w_out, b_out, gain_attn, shift_attn, w_up, b_up, w_down, b_down, gain_ffn, shift_ffn):
    factor = HD ** (-0.5)
    queries = low(low_back(matmul(inputs, w_query) + b_query)).reshape(LEN, HEADS, HD)
    keys_all = low(low_back(matmul(inputs, w_key))).reshape(LEN, HEADS, HD)
    values_all = low(low_back(matmul(inputs, w_value) + b_value)).reshape(LEN, HEADS, HD)
    scores = jnp.einsum('qhd,khd->hqk', queries, keys_all, precision=HIGHEST)
    scores = low_back(scores * factor)
    allowed = segments[:, None] == segments[None, :]
    scores = jnp.where(allowed[None], scores, -1e+30)
    attend = jax.nn.softmax(scores, axis=-1)
    context = jnp.einsum('hqk,khd->qhd', low(attend), values_all, precision=HIGHEST).reshape(LEN, D)
    context = low(low_back(context))
    hidden_one = inputs + low_back(matmul(context, w_out)) + b_out
    after_attn = normalize(hidden_one, gain_attn, shift_attn)
    upper = low_back(matmul(low(after_attn), w_up) + b_up)
    activated = low(jax.nn.gelu(upper, approximate=False))
    hidden_two = after_attn + low_back(matmul(activated, w_down)) + b_down
    return normalize(hidden_two, gain_ffn, shift_ffn)

def reference(tokens, segment_ids, w_query, w_key, w_value, b_query, b_value, w_out, b_out, gain_attn, shift_attn, w_up, b_up, w_down, b_down, gain_ffn, shift_ffn, cotangent):
    weights = tuple((member.astype(jnp.float32) for member in (w_query, w_key, w_value, b_query, b_value, w_out, b_out, gain_attn, shift_attn, w_up, b_up, w_down, b_down, gain_ffn, shift_ffn)))
    row_count = tokens.shape[0] // LEN
    inputs = tokens.astype(jnp.float32).reshape(row_count, LEN, D)
    segments = segment_ids.reshape(row_count, LEN)
    cotangents = cotangent.astype(jnp.float32).reshape(row_count, LEN, D)

    def one_row(totals, member):
        row_input, row_segments, row_cotangent = member

        def apply_row(row_value, *params):
            return encoder(row_value, row_segments, *params)
        result, pullback = jax.vjp(apply_row, row_input, *weights)
        grads = pullback(row_cotangent)
        totals = tuple((current + extra for current, extra in zip(totals, grads[1:])))
        return (totals, (result.astype(jnp.bfloat16), grads[0]))
    starting = tuple((jnp.zeros_like(member) for member in weights))
    totals, (outputs, grad_inputs) = lax.scan(one_row, starting, (inputs, segments, cotangents))
    return (outputs.reshape(tokens.shape[0], D), grad_inputs.reshape(tokens.shape[0], D), totals[0], totals[1], totals[2], totals[3], totals[4], totals[5], totals[6], totals[7], totals[8], totals[9], totals[10], totals[11], totals[12], totals[13], totals[14])
```

```python
from functools import partial

import jax
import jax.numpy as jnp
from jax import lax
from jax.experimental import pallas as pl
from jax.experimental.pallas import tpu as pltpu
from jax.sharding import PartitionSpec as P

HD = 64
LEN = 1024
EPSILON = 1e-05
MASKED = -1e30
SCALE = HD**-0.5
BLOCKS = 16
PAIR = 2 * HD
MIB = 1 << 20

RATE = 0.43
TERMS = (
    0.12126930983343633,
    0.12199507019903895,
    0.1037291362969846,
    0.11912425719127386,
    -0.03444926125853447,
    0.18241234969276796,
    -0.14954241308342106,
    0.035461460124125724,
)

F32 = jnp.float32
BF16 = jnp.bfloat16


def nn(left, right):
    return lax.dot_general(left, right, (((1,), (0,)), ((), ())), preferred_element_type=F32)


def nt(left, right):
    return lax.dot_general(left, right, (((1,), (1,)), ((), ())), preferred_element_type=F32)


def tn(left, right):
    return lax.dot_general(left, right, (((0,), (0,)), ((), ())), preferred_element_type=F32)


def normalize_parts(hidden):
    average = jnp.mean(hidden, axis=-1, keepdims=True)
    centred = hidden - average
    spread = jnp.mean(centred * centred, axis=-1, keepdims=True)
    inverse = lax.rsqrt(spread + EPSILON)
    return centred * inverse, inverse


def normalize_back(grad_out, normed, inverse, gain):
    scaled = grad_out * gain
    first_mean = jnp.mean(scaled, axis=-1, keepdims=True)
    second_mean = jnp.mean(scaled * normed, axis=-1, keepdims=True)
    return inverse * (scaled - first_mean - normed * second_mean)


def gelu_parts(upper):
    size = jnp.abs(upper) * (0.5**0.5)
    t = 1.0 / (1.0 + RATE * size)
    series = TERMS[-1] * t + TERMS[-2]
    for term in TERMS[-3::-1]:
        series = series * t + term
    bell = jnp.exp(upper * upper * -0.5)
    tail = series * t * bell
    phi = jnp.where(upper >= 0.0, 1.0 - tail, tail)
    return upper * phi, phi + upper * bell * 0.3989422804014327


def call(kernel, outs, ins, scratch=(), limit=48, smem=(), flops=0, moved=0):
    moved = moved or sum(a.size * a.dtype.itemsize for a in ins) + sum(
        o.size * o.dtype.itemsize for o in outs
    )
    return pl.pallas_call(
        kernel,
        out_shape=outs,
        in_specs=[
            pl.BlockSpec(memory_space=pltpu.SMEM if i in smem else pltpu.VMEM)
            for i in range(len(ins))
        ],
        out_specs=[pl.BlockSpec(memory_space=pltpu.VMEM) for _ in outs],
        scratch_shapes=list(scratch),
        compiler_params=pltpu.CompilerParams(vmem_limit_bytes=limit * MIB),
        cost_estimate=pl.CostEstimate(flops=flops, bytes_accessed=moved, transcendentals=0),
    )(*ins)


def shape(*dims, dtype=F32):
    return jax.ShapeDtypeStruct(dims, dtype)


def fill_bias(bias, segc_ref, segr_ref):
    bias[...] = jnp.where(segc_ref[...] == segr_ref[0], 0.0, MASKED)


def attend_kernel(
    x_ref, wq_ref, wk_ref, wv_ref, bq_ref, bv_ref, segr_ref, segc_ref,
    q_ref, k_ref, v_ref, ctx_ref, lse_ref,
    bias, vt, ctxt,
):
    heads = q_ref.shape[1] // HD
    block = 256
    x = x_ref[...]
    fill_bias(bias, segc_ref, segr_ref)
    q_ref[...] = ((nn(x, wq_ref[...]) + bq_ref[...]) * SCALE).astype(BF16)
    k_ref[...] = nn(x, wk_ref[...]).astype(BF16)
    value = (nn(x, wv_ref[...]) + bv_ref[...]).astype(BF16)
    v_ref[...] = value
    vt[...] = value.T

    @pl.loop(0, LEN // block)
    def _(j):
        here = pl.ds(pl.multiple_of(j * block, block), block)
        for pair in range(heads // 2):
            lanes = pl.ds(pair * PAIR, PAIR)
            keys = k_ref[:, lanes]
            queries = q_ref[here, lanes]
            owner = lax.broadcasted_iota(jnp.int32, queries.shape, 1) // HD
            for side in range(2):
                head = 2 * pair + side
                mine = jnp.where(owner == side, queries, jnp.zeros_like(queries))
                scores = nt(keys, mine) + bias[:, here]
                top = jnp.max(scores, axis=0, keepdims=True)
                weight = jnp.exp(scores - top)
                total = jnp.sum(weight, axis=0, keepdims=True)
                out = nn(vt[pl.ds(head * HD, HD), :], weight.astype(BF16))
                ctxt[pl.ds(head * HD, HD), here] = out * (1.0 / total)
                lse_ref[0, pl.ds(head, 1), here] = top + jnp.log(total)

    ctx_ref[...] = ctxt[...].T.astype(BF16)


def attention_forward(tokens, w_query, w_key, w_value, b_query, b_value, seg_rows, seg_cols):
    rows, width = seg_rows.shape[0], w_query.shape[1]
    model = tokens.shape[1]
    by_row = pl.BlockSpec((LEN, width), lambda r: (r, 0))
    whole = lambda *dims: pl.BlockSpec(dims, lambda r: (0,) * len(dims))
    flops = rows * (2 * LEN * model * 3 * width + 4 * 4 * LEN * LEN * width)
    return pl.pallas_call(
        attend_kernel,
        grid=(rows,),
        out_shape=[
            shape(rows * LEN, width, dtype=BF16),
            shape(rows * LEN, width, dtype=BF16),
            shape(rows * LEN, width, dtype=BF16),
            shape(rows * LEN, width, dtype=BF16),
            shape(rows, 8, LEN),
        ],
        in_specs=[
            pl.BlockSpec((LEN, model), lambda r: (r, 0)),
            whole(model, width),
            whole(model, width),
            whole(model, width),
            whole(1, width),
            whole(1, width),
            pl.BlockSpec((1, 1, LEN), lambda r: (r, 0, 0)),
            pl.BlockSpec((LEN, 1), lambda r: (r, 0)),
        ],
        out_specs=[by_row] * 4 + [pl.BlockSpec((1, 8, LEN), lambda r: (r, 0, 0))],
        scratch_shapes=[
            pltpu.VMEM((LEN, LEN), F32),
            pltpu.VMEM((width, LEN), BF16),
            pltpu.VMEM((width, LEN), F32),
        ],
        compiler_params=pltpu.CompilerParams(vmem_limit_bytes=40 * MIB),
        cost_estimate=pl.CostEstimate(flops=flops, bytes_accessed=8 * MIB, transcendentals=0),
    )(tokens, w_query, w_key, w_value, b_query, b_value, seg_rows, seg_cols)


def attend_back_kernel(
    q_ref, k_ref, v_ref, ctx_ref, dctx_ref, lse_ref, segr_ref, segc_ref,
    dq_ref, dk_ref, dv_ref,
    bias, kt, dqt, dk_sum, dv_sum, inner,
):
    width = q_ref.shape[1]
    heads = width // HD
    block = 256
    fill_bias(bias, segc_ref, segr_ref)
    kt[...] = k_ref[...].T
    picks = lax.broadcasted_iota(jnp.int32, (8, width), 0) == (
        lax.broadcasted_iota(jnp.int32, (8, width), 1) // HD
    )
    product = ctx_ref[...].astype(F32) * dctx_ref[...].astype(F32)
    inner[...] = lax.dot_general(
        picks.astype(F32), product, (((1,), (1,)), ((), ())),
        precision=lax.Precision.HIGHEST, preferred_element_type=F32,
    )
    dk_sum[...] = jnp.zeros_like(dk_sum)
    dv_sum[...] = jnp.zeros_like(dv_sum)

    @pl.loop(0, LEN // block)
    def _(j):
        here = pl.ds(pl.multiple_of(j * block, block), block)
        for pair in range(heads // 2):
            lanes = pl.ds(pair * PAIR, PAIR)
            keys, values = k_ref[:, lanes], v_ref[:, lanes]
            queries, grads = q_ref[here, lanes], dctx_ref[here, lanes]
            owner = lax.broadcasted_iota(jnp.int32, queries.shape, 1) // HD
            for side in range(2):
                head = 2 * pair + side
                query = jnp.where(owner == side, queries, jnp.zeros_like(queries))
                grad = jnp.where(owner == side, grads, jnp.zeros_like(grads))
                scores = nt(keys, query) + bias[:, here]
                weight = jnp.exp(scores - lse_ref[0, pl.ds(head, 1), here])
                slope = nt(values, grad) - inner[pl.ds(head, 1), here]
                change = (weight * slope).astype(BF16)
                dv_sum[:, lanes] += nn(weight.astype(BF16), grad)
                dk_sum[:, lanes] += nn(change, query)
                dqt[pl.ds(head * HD, HD), here] = nn(kt[pl.ds(head * HD, HD), :], change) * SCALE

    dq_ref[...] = dqt[...].T.astype(BF16)
    dk_ref[...] = dk_sum[...].astype(BF16)
    dv_ref[...] = dv_sum[...].astype(BF16)


def attention_backward(query, key, value, context, grad_context, lse, seg_rows, seg_cols):
    rows, width = seg_rows.shape[0], query.shape[1]
    by_row = pl.BlockSpec((LEN, width), lambda r: (r, 0))
    flops = rows * 4 * 10 * LEN * LEN * width
    return pl.pallas_call(
        attend_back_kernel,
        grid=(rows,),
        out_shape=[shape(rows * LEN, width, dtype=BF16)] * 3,
        in_specs=[by_row] * 5
        + [
            pl.BlockSpec((1, 8, LEN), lambda r: (r, 0, 0)),
            pl.BlockSpec((1, 1, LEN), lambda r: (r, 0, 0)),
            pl.BlockSpec((LEN, 1), lambda r: (r, 0)),
        ],
        out_specs=[by_row] * 3,
        scratch_shapes=[
            pltpu.VMEM((LEN, LEN), F32),
            pltpu.VMEM((width, LEN), BF16),
            pltpu.VMEM((width, LEN), F32),
            pltpu.VMEM((LEN, width), F32),
            pltpu.VMEM((LEN, width), F32),
            pltpu.VMEM((8, LEN), F32),
        ],
        compiler_params=pltpu.CompilerParams(vmem_limit_bytes=40 * MIB),
        cost_estimate=pl.CostEstimate(flops=flops, bytes_accessed=8 * MIB, transcendentals=0),
    )(query, key, value, context, grad_context, lse, seg_rows, seg_cols)


def pack_down(order, total, out_ref):
    part, _, wide = out_ref.shape
    size, cols = out_ref.shape[1] // BLOCKS, wide // 2
    for p in range(part):
        for place in range(BLOCKS):
            start = order[p, place] * (2 * size)
            for half in range(2):
                rows = pl.ds(pl.multiple_of(start + half * size, 8), size)
                out_ref[p, pl.ds(place * size, size), pl.ds(half * cols, cols)] = total[
                    rows, pl.ds(p * cols, cols)
                ].astype(BF16)


def pack_up(order, total, out_ref):
    part, _, cols = out_ref.shape
    size = out_ref.shape[1] // BLOCKS
    for p in range(part):
        for place in range(BLOCKS):
            rows = pl.ds(pl.multiple_of(order[p, place] * size, 8), size)
            out_ref[p, pl.ds(place * size, size), :] = total[
                rows, pl.ds(p * cols, cols)
            ].astype(BF16)


def forward_kernel(
    x_ref, ctx_a, ctx_b, wo_a, wo_b, b_out, gain_one, shift_one,
    wu_a, wu_b, bu_a, bu_b, wd_a, wd_b, b_down, gain_two, shift_two, cot_ref, order,
    mixed_ref, after_ref, normed_ref, inverse_ref, slope_a, slope_b, grad_ref, low_ref, sums_ref,
    down_a, down_b,
    act, total,
):
    half = wu_a.shape[1]
    chunk = 512
    hidden = (
        x_ref[...].astype(F32)
        + nn(ctx_a[...], wo_a[...])
        + nn(ctx_b[...], wo_b[...])
        + b_out[...]
    )
    normed, inverse = normalize_parts(hidden)
    normed_ref[...] = normed
    inverse_ref[...] = inverse
    after = normed * gain_one[...] + shift_one[...]
    after_low = after.astype(BF16)
    after_ref[...] = after_low
    second = after + b_down[...]
    for side, (wu, bu, wd, slope) in enumerate(
        ((wu_a, bu_a, wd_a, slope_a), (wu_b, bu_b, wd_b, slope_b))
    ):
        for start in range(0, half, chunk):
            here = pl.ds(start, chunk)
            upper = nn(after_low, wu[:, here]) + bu[:, here]
            active, steep = gelu_parts(upper)
            active = active.astype(BF16)
            slope[:, here] = steep.astype(BF16)
            act[:, pl.ds(side * half + start, chunk)] = active
            second = second + nn(active, wd[here, :])
    normed_two, inverse_two = normalize_parts(second)
    mixed_ref[...] = (normed_two * gain_two[...] + shift_two[...]).astype(BF16)
    outer = cot_ref[...].astype(F32)
    grad = normalize_back(outer, normed_two, inverse_two, gain_two[...])
    grad_ref[...] = grad
    low = grad.astype(BF16)
    low_ref[...] = low
    sums_ref[...] = jnp.zeros_like(sums_ref)
    sums_ref[0:1, :] = jnp.sum(outer * normed_two, axis=0, keepdims=True)
    sums_ref[1:2, :] = jnp.sum(outer, axis=0, keepdims=True)
    sums_ref[2:3, :] = jnp.sum(grad, axis=0, keepdims=True)
    for side, out_ref in ((1, down_b), (0, down_a)):
        for start in range(0, half, chunk):
            total[pl.ds(start, chunk), :] = tn(act[:, pl.ds(side * half + start, chunk)], low)
        pack_down(order, total, out_ref)


def upper_kernel(
    low_ref, wd_a, wd_b, slope_a, slope_b, after_ref, order,
    gu_a, gu_b, sum_a, sum_b, up_a, up_b,
    total,
):
    half = wd_a.shape[0]
    chunk = 512
    low, after = low_ref[...], after_ref[...]
    for wd, slope, gu, sums, out_ref in (
        (wd_b, slope_b, gu_b, sum_b, up_b),
        (wd_a, slope_a, gu_a, sum_a, up_a),
    ):
        for start in range(0, half, chunk):
            here = pl.ds(start, chunk)
            grad = (nt(low, wd[here, :]) * slope[:, here].astype(F32)).astype(BF16)
            gu[:, here] = grad
            sums[:, here] = jnp.sum(grad.astype(F32), axis=0, keepdims=True)
            total[:, here] = tn(after, grad)
        pack_up(order, total, out_ref)


def first_norm_kernel(
    gu_a, gu_b, wu_a, wu_b, grad_ref, normed_ref, inverse_ref, gain_one, wo_a, wo_b, ctx_a, ctx_b,
    grad_one_ref, sums_ref, gctx_a, gctx_b, out_a, out_b,
):
    width = ctx_a.shape[1]
    after = grad_ref[...] + nt(gu_a[...], wu_a[...]) + nt(gu_b[...], wu_b[...])
    normed = normed_ref[...]
    grad = normalize_back(after, normed, inverse_ref[...], gain_one[...])
    grad_one_ref[...] = grad
    low = grad.astype(BF16)
    gctx_b[...] = nt(low, wo_b[...]).astype(BF16)
    gctx_a[...] = nt(low, wo_a[...]).astype(BF16)
    sums_ref[...] = jnp.zeros_like(sums_ref)
    sums_ref[0:1, :] = jnp.sum(after * normed, axis=0, keepdims=True)
    sums_ref[1:2, :] = jnp.sum(after, axis=0, keepdims=True)
    sums_ref[2:3, :] = jnp.sum(grad, axis=0, keepdims=True)
    for ctx, out_ref in ((ctx_b, out_b), (ctx_a, out_a)):
        both = tn(ctx[...], low).astype(BF16)
        out_ref[pl.ds(0, width), :] = both[:, :width]
        out_ref[pl.ds(width, width), :] = both[:, width:]


def project_kernel(
    x_ref, dq_ref, dk_ref, dv_ref, out_a, out_b, order, packed, sum_q, sum_v, total, both
):
    width = dq_ref.shape[1]
    size = packed.shape[1] // BLOCKS
    cols = width // 3
    x = x_ref[...]
    sum_q[...] = jnp.sum(dq_ref[...].astype(F32), axis=0, keepdims=True)
    sum_v[...] = jnp.sum(dv_ref[...].astype(F32), axis=0, keepdims=True)
    both[...] = out_a[...].astype(F32) + out_b[...].astype(F32)
    for p, grad in enumerate((dq_ref, dk_ref, dv_ref)):
        total[...] = tn(x, grad[...])
        for place in range(BLOCKS):
            rows = pl.ds(pl.multiple_of(order[p, place] * size, 8), size)
            to = pl.ds(place * size, size)
            packed[p, to, pl.ds(0, width)] = total[rows, :].astype(BF16)
            packed[p, to, pl.ds(width, cols)] = both[rows, pl.ds(p * cols, cols)].astype(BF16)


def unpack_down_kernel(a_ref, b_ref, c_ref, order, out_ref):
    size, cols = a_ref.shape[0] // BLOCKS, a_ref.shape[1] // 2
    for p, ref in enumerate((a_ref, b_ref, c_ref)):
        for place in range(BLOCKS):
            start = order[p, place] * (2 * size)
            for half in range(2):
                rows = pl.ds(pl.multiple_of(start + half * size, 8), size)
                out_ref[rows, pl.ds(p * cols, cols)] = ref[
                    pl.ds(place * size, size), pl.ds(half * cols, cols)
                ].astype(F32)


def unpack_up_kernel(a_ref, b_ref, c_ref, order, out_ref):
    size, cols = a_ref.shape[0] // BLOCKS, a_ref.shape[1]
    for p, ref in enumerate((a_ref, b_ref, c_ref)):
        for place in range(BLOCKS):
            rows = pl.ds(pl.multiple_of(order[p, place] * size, 8), size)
            out_ref[rows, pl.ds(p * cols, cols)] = ref[pl.ds(place * size, size), :].astype(F32)


def unpack_project_kernel(a_ref, b_ref, c_ref, order, q_ref, k_ref, v_ref, out_ref):
    width = q_ref.shape[1]
    size, cols = a_ref.shape[0] // BLOCKS, width // 3
    for p, (ref, grad) in enumerate(((a_ref, q_ref), (b_ref, k_ref), (c_ref, v_ref))):
        for place in range(BLOCKS):
            which = order[p, place]
            rows = pl.ds(pl.multiple_of(which * size, 8), size)
            grad[rows, :] = ref[pl.ds(place * size, size), pl.ds(0, width)].astype(F32)
            left = ref[pl.ds(place * size, size), pl.ds(width, cols)].astype(F32)
            rows = pl.ds(pl.multiple_of(lax.rem(which, BLOCKS // 2) * size, 8), size)
            at = pl.multiple_of(lax.div(which, BLOCKS // 2) * width + p * cols, 128)
            out_ref[rows, pl.ds(at, cols)] = left


def swap(value, bit, count):
    return lax.ppermute(value, "dp", [(i, i ^ bit) for i in range(count)])


def across(value):
    return lax.ppermute(value, "tensor", [(0, 1), (1, 0)])


def add(left, right):
    return (left.astype(F32) + right.astype(F32)).astype(BF16)


STAGES = ((1, 2, 4, 8), (2, 4, 1, 8), (4, 1, 2, 8))


def block_order():
    mine = lax.rem(lax.axis_index("dp"), BLOCKS // 2)
    rows = []
    for bits in STAGES:
        rows.append(
            [
                sum(bit for i, bit in enumerate(bits) if place >> (len(bits) - 1 - i) & 1)
                for place in range(BLOCKS)
            ]
        )
    return jnp.bitwise_xor(jnp.array(rows, jnp.int32), mine.astype(jnp.int32))


def sum_over_dp(own, other, count):
    results = []
    for p, bits in enumerate(STAGES):
        half = own[p].shape[0] // 2
        keep = add(own[p][:half], other[p][:half]) if other is not None else own[p][:half]
        send = add(own[p][half:], other[p][half:]) if other is not None else own[p][half:]
        for step in range(3):
            got = swap(send, bits[step], count)
            both = add(keep, got)
            half //= 2
            if step < 2:
                keep, send = both[:half], both[half:]
        extra = BLOCKS // 2
        while extra < count:
            both = add(both, swap(both, extra, count))
            extra *= 2
        for step in (2, 1, 0):
            both = jnp.concatenate([both, swap(both, bits[step], count)], axis=0)
        results.append(both)
    return results


def shards(
    tokens, segment_ids, w_query, w_key, w_value, b_query, b_value, w_out, b_out, gain_attn,
    shift_attn, w_up, b_up, w_down, b_down, gain_ffn, shift_ffn, cotangent,
):
    count = lax.axis_size("dp")
    here, model = tokens.shape
    width, half = w_query.shape[1], w_up.shape[1]
    row = lambda vector: vector.reshape(1, -1)

    tokens_b = across(tokens)
    segments_b = across(segment_ids)
    wo_b, wu_b, bu_b, wd_b = across(w_out), across(w_up), across(b_up), across(w_down)
    order = block_order()

    inputs = jnp.concatenate([tokens, tokens_b], axis=0)
    segments = jnp.concatenate([segment_ids, segments_b], axis=0)
    rows = inputs.shape[0] // LEN
    seg_rows, seg_cols = segments.reshape(rows, 1, LEN), segments.reshape(rows * LEN, 1)
    query, key, value, context, lse = attention_forward(
        inputs, w_query, w_key, w_value, row(b_query), row(b_value), seg_rows, seg_cols
    )
    ctx_a, ctx_b = context[:here], across(context[here:])

    parts = shape(3, model, half // 3, dtype=BF16)
    (
        mixed, after_low, normed_one, inverse_one, slope_a, slope_b, grad_two, grad_two_low, sums_two,
        down_a, down_b,
    ) = call(
        forward_kernel,
        [
            shape(here, model, dtype=BF16),
            shape(here, model, dtype=BF16),
            shape(here, model),
            shape(here, 1),
            shape(here, half, dtype=BF16),
            shape(here, half, dtype=BF16),
            shape(here, model),
            shape(here, model, dtype=BF16),
            shape(8, model),
            parts,
            parts,
        ],
        [
            tokens, ctx_a, ctx_b, w_out, wo_b, row(b_out), row(gain_attn), row(shift_attn),
            w_up, wu_b, row(b_up), row(bu_b), w_down, wd_b, row(b_down), row(gain_ffn),
            row(shift_ffn), cotangent, order,
        ],
        [pltpu.VMEM((here, 2 * half), BF16), pltpu.VMEM((half, model), F32)],
        limit=56,
        smem=(18,),
        flops=2 * here * model * (2 * width + 6 * half),
    )
    down_got = across(down_b)

    gu_a, gu_b, sum_up_a, sum_up_b, up_a, up_b = call(
        upper_kernel,
        [
            shape(here, half, dtype=BF16),
            shape(here, half, dtype=BF16),
            shape(1, half),
            shape(1, half),
            parts,
            parts,
        ],
        [grad_two_low, w_down, wd_b, slope_a, slope_b, after_low, order],
        [pltpu.VMEM((model, half), F32)],
        smem=(6,),
        flops=2 * here * model * 4 * half,
    )
    up_got = across(up_b)

    grad_one, sums_one, gctx_a, gctx_b, out_a, out_b = call(
        first_norm_kernel,
        [
            shape(here, model),
            shape(8, model),
            shape(here, width, dtype=BF16),
            shape(here, width, dtype=BF16),
            shape(model, width, dtype=BF16),
            shape(model, width, dtype=BF16),
        ],
        [
            gu_a, gu_b, w_up, wu_b, grad_two, normed_one, inverse_one, row(gain_attn),
            w_out, wo_b, ctx_a, ctx_b,
        ],
        flops=2 * here * model * (2 * half + 4 * width),
    )
    grad_context = jnp.concatenate([gctx_a, across(gctx_b)], axis=0)
    out_got = across(out_b)

    dq, dk, dv = attention_backward(
        query, key, value, context, grad_context, lse, seg_rows, seg_cols
    )
    packed, sum_q, sum_v = call(
        project_kernel,
        [parts, shape(1, width), shape(1, width)],
        [inputs, dq, dk, dv, out_a, out_got, order],
        [pltpu.VMEM((model, width), F32), pltpu.VMEM((model, width), F32)],
        smem=(6,),
        flops=2 * 2 * here * model * 3 * width,
    )

    def to_tokens(part):
        return nt(dq[part], w_query) + nt(dk[part], w_key) + nt(dv[part], w_value)

    token_got = across(to_tokens(slice(here, None)).astype(BF16))
    grad_tokens = to_tokens(slice(0, here)) + token_got.astype(F32) + grad_one

    downs = sum_over_dp(down_a, down_got, count)
    ups = sum_over_dp(up_a, up_got, count)
    projects = sum_over_dp(packed, None, count)
    (grad_w_down,) = call(
        unpack_down_kernel, [shape(half, model)], [*downs, order], limit=32, smem=(3,)
    )
    (grad_w_up,) = call(
        unpack_up_kernel, [shape(model, half)], [*ups, order], limit=32, smem=(3,)
    )
    grad_w_query, grad_w_key, grad_w_value, grad_w_out = call(
        unpack_project_kernel,
        [shape(model, width)] * 3 + [shape(width, model)],
        [*projects, order],
        limit=32,
        smem=(3,),
    )

    sums_up = sum_up_a + across(sum_up_b)
    shared = jnp.concatenate([sums_one[:3], sums_two[:3]], axis=0)
    shared = (shared + across(shared)).reshape(-1)
    small = jnp.concatenate([shared, sum_q[0], sum_v[0], sums_up[0]]).reshape(-1, 128)
    bit = 1
    while bit < count:
        small = small + swap(small, bit, count)
        bit *= 2
    small = small.reshape(-1)
    cuts = [model * i for i in range(1, 7)] + [6 * model + width, 6 * model + 2 * width]
    (
        grad_gain_attn, grad_shift_attn, grad_b_out, grad_gain_ffn, grad_shift_ffn, grad_b_down,
        grad_b_query, grad_b_value, grad_b_up,
    ) = jnp.split(small, cuts)
    return (
        mixed, grad_tokens, grad_w_query, grad_w_key, grad_w_value, grad_b_query, grad_b_value,
        grad_w_out, grad_b_out, grad_gain_attn, grad_shift_attn, grad_w_up, grad_b_up, grad_w_down,
        grad_b_down, grad_gain_ffn, grad_shift_ffn,
    )


def solution(mesh):
    placed = (
        P(("dp", "tensor"), None),
        P(("dp", "tensor")),
        P(None, "tensor"),
        P(None, "tensor"),
        P(None, "tensor"),
        P("tensor"),
        P("tensor"),
        P("tensor", None),
        P(),
        P(),
        P(),
        P(None, "tensor"),
        P("tensor"),
        P("tensor", None),
        P(),
        P(),
        P(),
        P(("dp", "tensor"), None),
    )
    return jax.shard_map(
        shards,
        mesh=mesh,
        in_specs=placed,
        out_specs=(
            P(("dp", "tensor"), None),
            P(("dp", "tensor"), None),
            P(None, "tensor"),
            P(None, "tensor"),
            P(None, "tensor"),
            P("tensor"),
            P("tensor"),
            P("tensor", None),
            P(),
            P(),
            P(),
            P(None, "tensor"),
            P("tensor"),
            P("tensor", None),
            P(),
            P(),
            P(),
        ),
        check_vma=False,
    )
```

```python
from functools import partial

import jax
import jax.numpy as jnp
from jax import lax
from jax.experimental import pallas as pl
from jax.experimental.pallas import tpu as pltpu
from jax.sharding import PartitionSpec as P

HD = 64
LEN = 1024
EPSILON = 1e-05
MASKED = -1e30
SCALE = HD**-0.5
BLOCKS = 16
PAIR = 2 * HD
MIB = 1 << 20

F32 = jnp.float32
BF16 = jnp.bfloat16


def nn(left, right):
    return lax.dot_general(left, right, (((1,), (0,)), ((), ())), preferred_element_type=F32)


def nt(left, right):
    return lax.dot_general(left, right, (((1,), (1,)), ((), ())), preferred_element_type=F32)


def tn(left, right):
    return lax.dot_general(left, right, (((0,), (0,)), ((), ())), preferred_element_type=F32)


def normalize_parts(hidden):
    average = jnp.mean(hidden, axis=-1, keepdims=True)
    centred = hidden - average
    spread = jnp.mean(centred * centred, axis=-1, keepdims=True)
    inverse = lax.rsqrt(spread + EPSILON)
    return centred * inverse, inverse


def normalize_back(grad_out, normed, inverse, gain):
    scaled = grad_out * gain
    first_mean = jnp.mean(scaled, axis=-1, keepdims=True)
    second_mean = jnp.mean(scaled * normed, axis=-1, keepdims=True)
    return inverse * (scaled - first_mean - normed * second_mean)


def gelu_parts(upper):
    phi = 0.5 + 0.5 * lax.erf(upper * 0.5**0.5)
    bell = jnp.exp(upper * upper * -0.5)
    return upper * phi, phi + upper * bell * 0.3989422804014327


def lasting(us):
    return pl.CostEstimate(flops=int(us * 1.15e9), bytes_accessed=0, transcendentals=0)


def call(kernel, outs, ins, scratch=(), limit=48, smem=(), hbm=(), hbm_outs=(), us=5):
    place = lambda i, far: pl.BlockSpec(memory_space=pl.ANY if i in far else pltpu.VMEM)
    return pl.pallas_call(
        kernel,
        out_shape=outs,
        in_specs=[
            pl.BlockSpec(memory_space=pltpu.SMEM) if i in smem else place(i, hbm)
            for i in range(len(ins))
        ],
        out_specs=[place(i, hbm_outs) for i in range(len(outs))],
        scratch_shapes=list(scratch),
        compiler_params=pltpu.CompilerParams(vmem_limit_bytes=limit * MIB),
        cost_estimate=lasting(us),
    )(*ins)


def shape(*dims, dtype=F32):
    return jax.ShapeDtypeStruct(dims, dtype)


def as_row(ref):
    return ref[...].reshape(1, -1)


def join_segments(refs):
    return jnp.concatenate([as_row(ref).astype(F32) for ref in refs], axis=1)


def as_column(row):
    return jnp.broadcast_to(row, (8, row.shape[1])).T[:, :1]


def pairs(heads):
    return [pl.ds(pair * PAIR, PAIR) for pair in range(heads // 2)]


def split_pair(block):
    owner = lax.broadcasted_iota(jnp.int32, block.shape, 1) // HD
    empty = jnp.zeros_like(block)
    return jnp.concatenate(
        [jnp.where(owner == 0, block, empty), jnp.where(owner == 1, block, empty)], axis=0
    )


def attend_kernel(*refs, split):
    xs, refs = refs[:split], refs[split:]
    segs, refs = refs[:split], refs[split:]
    wq_ref, wk_ref, wv_ref, bq_ref, bv_ref = refs[:5]
    q_ref, k_ref, v_ref, *ctx_refs, lse_ref, bias, vt, ctxt = refs[5:]
    heads = q_ref.shape[1] // HD
    block = 256
    segments = join_segments(segs)
    bias[...] = jnp.where(as_column(segments) == segments, 0.0, MASKED)
    size = LEN // split
    for i, x_ref in enumerate(xs):
        x, rows = x_ref[...], pl.ds(i * size, size)
        q_ref[rows, :] = ((nn(x, wq_ref[...]) + as_row(bq_ref)) * SCALE).astype(BF16)
        k_ref[rows, :] = nn(x, wk_ref[...]).astype(BF16)
        value = (nn(x, wv_ref[...]) + as_row(bv_ref)).astype(BF16)
        v_ref[rows, :] = value
        vt[:, rows] = value.T

    @pl.loop(0, LEN // block)
    def _(j):
        here = pl.ds(pl.multiple_of(j * block, block), block)
        products = [
            nt(k_ref[:, lanes], split_pair(q_ref[here, lanes])) for lanes in pairs(heads)
        ]
        mask = bias[:, here]
        weights, tops, totals = [], [], []
        for head in range(heads):
            start = head % 2 * block
            scores = products[head // 2][:, start : start + block] + mask
            tops.append(jnp.max(scores, axis=0, keepdims=True))
            weight = jnp.exp(scores - tops[-1])
            totals.append(jnp.sum(weight, axis=0, keepdims=True))
            weights.append(weight.astype(BF16))
        for head in range(heads):
            at = pl.ds(head * HD, HD)
            ctxt[at, here] = nn(vt[at, :], weights[head]) * (1.0 / totals[head])
            lse_ref[0, pl.ds(head, 1), here] = tops[head] + jnp.log(totals[head])

    for i, ctx_ref in enumerate(ctx_refs):
        ctx_ref[...] = ctxt[:, pl.ds(i * size, size)].T.astype(BF16)


def attention_forward(xs, segs, w_query, w_key, w_value, b_query, b_value):
    split = len(xs)
    size = LEN // split
    rows, model = xs[0].shape[0] // size, xs[0].shape[1]
    width = w_query.shape[1]
    by_row = pl.BlockSpec((LEN, width), lambda r: (r, 0))
    by_part = pl.BlockSpec((size, width), lambda r: (r, 0))
    whole = lambda *dims: pl.BlockSpec(dims, lambda r: (0,) * len(dims))
    us = 13 * rows
    query, key, value, *contexts, lse = pl.pallas_call(
        partial(attend_kernel, split=split),
        grid=(rows,),
        out_shape=[shape(rows * LEN, width, dtype=BF16)] * 3
        + [shape(rows * size, width, dtype=BF16)] * split
        + [shape(rows, 8, LEN)],
        in_specs=[pl.BlockSpec((size, model), lambda r: (r, 0))] * split
        + [pl.BlockSpec((size,), lambda r: (r,))] * split
        + [
            whole(model, width),
            whole(model, width),
            whole(model, width),
            whole(width),
            whole(width),
        ],
        out_specs=[by_row] * 3
        + [by_part] * split
        + [pl.BlockSpec((1, 8, LEN), lambda r: (r, 0, 0))],
        scratch_shapes=[
            pltpu.VMEM((LEN, LEN), F32),
            pltpu.VMEM((width, LEN), BF16),
            pltpu.VMEM((width, LEN), F32),
        ],
        compiler_params=pltpu.CompilerParams(vmem_limit_bytes=60 * MIB),
        cost_estimate=lasting(us),
    )(*xs, *segs, w_query, w_key, w_value, b_query, b_value)
    return query, key, value, contexts, lse


def attend_back_kernel(
    q_ref, k_ref, v_ref, lse_ref, *refs, pair, split
):
    segs, ctx_refs, dctx_refs = (refs[i * split : (i + 1) * split] for i in range(3))
    dq_ref, dk_ref, dv_ref, kt, dqt, dk_sum, dv_sum, inner, dctx_ref, ctx_ref, seg = refs[
        3 * split :
    ]
    size = LEN // split
    for i in range(split):
        dctx_ref[pl.ds(i * size, size), :] = dctx_refs[i][...]
        ctx_ref[pl.ds(i * size, size), :] = ctx_refs[i][...]
    width = q_ref.shape[1]
    block = 256
    kt[...] = k_ref[...].T
    seg[...] = join_segments(segs)
    column = as_column(seg[...])
    picks = lax.broadcasted_iota(jnp.int32, (8, width), 0) == (
        lax.broadcasted_iota(jnp.int32, (8, width), 1) // HD
    )
    product = ctx_ref[...].astype(F32) * dctx_ref[...].astype(F32)
    inner[...] = lax.dot_general(
        picks.astype(F32), product, (((1,), (1,)), ((), ())),
        precision=lax.Precision.HIGHEST, preferred_element_type=F32,
    )
    dk_sum[...] = jnp.zeros_like(dk_sum)
    dv_sum[...] = jnp.zeros_like(dv_sum)

    @pl.loop(0, LEN // block)
    def _(j):
        here = pl.ds(pl.multiple_of(j * block, block), block)
        allowed = column == seg[:, here]
        queries, grads = split_pair(q_ref[here, :]), split_pair(dctx_ref[here, :])
        products, slopes = nt(k_ref[...], queries), nt(v_ref[...], grads)
        weights, changes = [], []
        for side in range(2):
            at = slice(side * block, (side + 1) * block)
            scores = jnp.where(allowed, products[:, at], MASKED)
            weight = jnp.exp(scores - lse_ref[0, 2 * pair + side : 2 * pair + side + 1, here])
            change = weight * (slopes[:, at] - inner[side : side + 1, here])
            weights.append(weight.astype(BF16))
            changes.append(change.astype(BF16))
        dv_sum[...] += nn(jnp.concatenate(weights, axis=1), grads)
        dk_sum[...] += nn(jnp.concatenate(changes, axis=1), queries)
        for side in range(2):
            at = slice(side * HD, (side + 1) * HD)
            dqt[at, here] = nn(kt[at, :], changes[side]) * SCALE

    dq_ref[...] = dqt[...].T.astype(BF16)
    dk_ref[...] = dk_sum[...].astype(BF16)
    dv_ref[...] = dv_sum[...].astype(BF16)


def attention_backward(pair, query, key, value, contexts, grads, lse, segs):
    rows, split = query.shape[0] // LEN, len(contexts)
    columns = pl.BlockSpec((LEN, PAIR), lambda r: (r, pair))
    part = pl.BlockSpec((LEN // split, PAIR), lambda r: (r, pair))
    own = pl.BlockSpec((LEN, PAIR), lambda r: (r, 0))
    us = 7 * rows
    return pl.pallas_call(
        partial(attend_back_kernel, pair=pair, split=split),
        grid=(rows,),
        out_shape=[shape(rows * LEN, PAIR, dtype=BF16)] * 3,
        in_specs=[columns] * 3
        + [
            pl.BlockSpec((1, 8, LEN), lambda r: (r, 0, 0)),
        ]
        + [pl.BlockSpec((LEN // split,), lambda r: (r,))] * split
        + [part] * (2 * split),
        out_specs=[own] * 3,
        scratch_shapes=[
            pltpu.VMEM((PAIR, LEN), BF16),
            pltpu.VMEM((PAIR, LEN), F32),
            pltpu.VMEM((LEN, PAIR), F32),
            pltpu.VMEM((LEN, PAIR), F32),
            pltpu.VMEM((8, LEN), F32),
            pltpu.VMEM((LEN, PAIR), BF16),
            pltpu.VMEM((LEN, PAIR), BF16),
            pltpu.VMEM((1, LEN), F32),
        ],
        compiler_params=pltpu.CompilerParams(vmem_limit_bytes=24 * MIB),
        cost_estimate=lasting(us),
    )(query, key, value, lse, *segs, *contexts, *grads)


def rearrange(order, part, source, target):
    size = source.shape[0] // BLOCKS
    for place in range(BLOCKS):
        rows = pl.ds(pl.multiple_of(order[part, place] * size, 16), size)
        target[pl.ds(place * size, size), :] = source[rows, :]


class Copies:
    def __init__(self, sems):
        self.sems, self.used, self.open = sems, 0, []

    def start(self, source, target):
        copy = pltpu.make_async_copy(source, target, self.sems.at[self.used])
        self.used += 1
        copy.start()
        return copy

    def store(self, source, target):
        self.open.append(self.start(source, target))

    def drain(self):
        for copy in self.open:
            copy.wait()


STRIP = 512


def fold(rows):
    return sum(rows[i : i + 8, :] for i in range(0, rows.shape[0], 8))


def put_sums(sums_ref, sums):
    sums_ref[...] = jnp.zeros_like(sums_ref)
    for i, part in enumerate(sums):
        sums_ref[i : i + 1, :] = jnp.sum(part, axis=0, keepdims=True)


def forward_kernel(
    x_ref, ctx_a, ctx_b, wo_a, wo_b, b_out, gain_one, shift_one, b_down, gain_two, shift_two,
    bu_a, bu_b, order, wu_a, wu_b, wd_a, wd_b, cot_hbm,
    inverse_ref, sums_ref, mixed_hbm, after_hbm, normed_hbm, slope_hbm, grad_hbm, low_hbm,
    down_b, moved_hbm, act_hbm,
    wu, wd, cot, mixed, after_buf, normed_buf, slope, grad_buf, low_buf, act, flipped, moved, parts,
    total, sems,
):
    half = wu_a.shape[1]
    chunk = 512
    copies = Copies(sems)
    ups, downs = [], []
    for side, (up, down) in enumerate(((wu_a, wd_a), (wu_b, wd_b))):
        for start in range(0, half, chunk):
            to = pl.ds(side * half + start, chunk)
            ups.append(copies.start(up.at[:, pl.ds(start, chunk)], wu.at[:, to]))
            downs.append(copies.start(down.at[pl.ds(start, chunk), :], wd.at[to, :]))
    cot_copy = copies.start(cot_hbm, cot)
    b_out, gain_one, shift_one, b_down, gain_two, shift_two = map(
        as_row, (b_out, gain_one, shift_one, b_down, gain_two, shift_two)
    )
    biases = [as_row(bu_a), as_row(bu_b)]
    total[...] = nn(ctx_a[...], wo_a[...]) + nn(ctx_b[...], wo_b[...])

    @pl.loop(0, x_ref.shape[0] // STRIP)
    def _(i):
        rows = pl.ds(pl.multiple_of(i * STRIP, STRIP), STRIP)
        normed, inverse = normalize_parts(x_ref[rows, :].astype(F32) + total[rows, :] + b_out)
        normed_buf[rows, :] = normed
        inverse_ref[rows, :] = inverse
        after_buf[rows, :] = (normed * gain_one + shift_one).astype(BF16)

    copies.store(normed_buf, normed_hbm)
    copies.store(after_buf, after_hbm)
    after_low = after_buf[...]

    def raise_up(i):
        ups[i].wait()
        here = pl.ds(i * chunk, chunk)
        start = i * chunk % half
        return nn(after_low, wu[:, here]) + biases[i * chunk // half][:, start : start + chunk]

    count = 2 * half // chunk
    upper = raise_up(0)
    for i in range(count):
        following = raise_up(i + 1) if i + 1 < count else None
        here = pl.ds(i * chunk, chunk)
        active, steep = gelu_parts(upper)
        act[:, here] = active.astype(BF16)
        slope[:, here] = steep.astype(BF16)
        copies.store(slope.at[:, here], slope_hbm.at[:, here])
        upper = following
    for copy in downs:
        copy.wait()
    total[...] = nn(act[...], wd[...])
    cot_copy.wait()

    def finish(i, sums):
        rows = pl.ds(pl.multiple_of(i * STRIP, STRIP), STRIP)
        after = normed_buf[rows, :] * gain_one + shift_one
        normed, inverse = normalize_parts(after + total[rows, :] + b_down)
        mixed[rows, :] = (normed * gain_two + shift_two).astype(BF16)
        outer = cot[rows, :].astype(F32)
        grad = normalize_back(outer, normed, inverse, gain_two)
        grad_buf[rows, :] = grad
        low_buf[rows, :] = grad.astype(BF16)
        return tuple(
            held + fold(extra) for held, extra in zip(sums, (outer * normed, outer, grad))
        )

    empty = jnp.zeros((8, x_ref.shape[1]), F32)
    sums = lax.fori_loop(0, x_ref.shape[0] // STRIP, finish, (empty, empty, empty))
    copies.store(mixed, mixed_hbm)
    copies.store(grad_buf, grad_hbm)
    copies.store(low_buf, low_hbm)
    flipped[...] = grad_buf[...].T.astype(BF16)
    put_sums(sums_ref, sums)
    cols = half // 3
    for p in range(3):
        rearrange(order, p, flipped, moved.at[p])
    for p in range(3):
        here = pl.ds(half + p * cols, cols)
        parts[p] = nn(moved[p], act[:, here]).astype(BF16)
        copies.store(parts.at[p], down_b.at[p])
    copies.store(moved, moved_hbm)
    copies.store(act.at[:, pl.ds(0, half)], act_hbm)
    copies.drain()


def upper_kernel(
    order, low_hbm, after_hbm, moved_hbm, act_hbm, slope_hbm, wd_a, wd_b,
    sums, gu_hbm, down_a, up_a, up_b,
    wd, slope, gu, low_ref, after_ref, grad_moved, act_ref, flipped, moved, parts, sems,
):
    half = wd_a.shape[0]
    cols = half // 3
    copies = Copies(sems)
    slopes, downs = {}, {}
    low_copy = copies.start(low_hbm, low_ref)
    after_copy = copies.start(after_hbm, after_ref)
    for side, down in ((1, wd_b), (0, wd_a)):
        for p in range(3):
            to = pl.ds(side * half + p * cols, cols)
            downs[side, p] = copies.start(down.at[pl.ds(p * cols, cols), :], wd.at[to, :])
            slopes[side, p] = copies.start(slope_hbm.at[:, to], slope.at[:, to])
    rest = [copies.start(moved_hbm, grad_moved), copies.start(act_hbm, act_ref)]
    low_copy.wait()
    after_copy.wait()
    low = low_ref[...]
    flipped[...] = after_ref[...].T
    for p in range(3):
        rearrange(order, p, flipped, moved.at[p])

    def pull(side, p):
        downs[side, p].wait()
        return nt(low, wd[pl.ds(side * half + p * cols, cols), :])

    todo = [(side, p) for side in (1, 0) for p in range(3)]
    pulled = pull(*todo[0])
    for i, (side, p) in enumerate(todo):
        following = pull(*todo[i + 1]) if i + 1 < len(todo) else None
        here = pl.ds(side * half + p * cols, cols)
        slopes[side, p].wait()
        gu[:, here] = (pulled * slope[:, here].astype(F32)).astype(BF16)
        copies.store(gu.at[:, here], gu_hbm.at[:, here])
        grad = gu[:, here]
        sums[:, here] = jnp.sum(grad.astype(F32), axis=0, keepdims=True)
        parts[side, p] = nn(moved[p], grad).astype(BF16)
        copies.store(parts.at[side, p], (up_b if side else up_a).at[p])
        pulled = following
    for copy in rest:
        copy.wait()
    for p in range(3):
        parts[2, p] = nn(grad_moved[p], act_ref[:, pl.ds(p * cols, cols)]).astype(BF16)
        copies.store(parts.at[2, p], down_a.at[p])
    copies.drain()


def first_norm_kernel(
    inverse_ref, gain_ref, order, wo_a, wo_b, ctx_a, ctx_b, grad_hbm, normed_hbm, gu_hbm, wu_a, wu_b,
    sums_ref, gctx_a, gctx_b, out_a, out_b, grad_one_hbm,
    gu, wu, grad_buf, normed_buf, one, acc, low_buf, flipped, moved, sems,
):
    half = wu_a.shape[1]
    chunk = 512
    copies = Copies(sems)
    pending = []
    for side, up in enumerate((wu_a, wu_b)):
        for start in range(0, half, chunk):
            to = pl.ds(side * half + start, chunk)
            pending.append(
                (
                    copies.start(gu_hbm.at[:, to], gu.at[:, to]),
                    copies.start(up.at[:, pl.ds(start, chunk)], wu.at[:, to]),
                )
            )
    grad_copy = copies.start(grad_hbm, grad_buf)
    normed_copy = copies.start(normed_hbm, normed_buf)
    step = half // chunk
    for side in range(2):
        for first, second in pending[side * step : (side + 1) * step]:
            first.wait()
            second.wait()
        at = pl.ds(side * half, half)
        term = nt(gu[:, at], wu[:, at])
        acc[...] = term if side == 0 else acc[...] + term
    grad_copy.wait()
    normed_copy.wait()
    gain = as_row(gain_ref)

    def finish(i, sums):
        rows = pl.ds(pl.multiple_of(i * STRIP, STRIP), STRIP)
        after = grad_buf[rows, :] + acc[rows, :]
        normed = normed_buf[rows, :]
        grad = normalize_back(after, normed, inverse_ref[rows, :], gain)
        one[rows, :] = grad
        low_buf[rows, :] = grad.astype(BF16)
        return tuple(
            held + fold(extra) for held, extra in zip(sums, (after * normed, after, grad))
        )

    empty = jnp.zeros((8, one.shape[1]), F32)
    sums = lax.fori_loop(0, one.shape[0] // STRIP, finish, (empty, empty, empty))
    copies.store(one, grad_one_hbm)
    low = low_buf[...]
    gctx_b[...] = nt(low, wo_b[...]).astype(BF16)
    gctx_a[...] = nt(low, wo_a[...]).astype(BF16)
    flipped[...] = one[...].T.astype(BF16)
    put_sums(sums_ref, sums)
    cols = ctx_a.shape[1] // 3
    for p in range(3):
        rearrange(order, p, flipped, moved)
        here = pl.ds(p * cols, cols)
        out_b[p] = nn(moved[...], ctx_b[:, here]).astype(BF16)
        out_a[p] = nn(moved[...], ctx_a[:, here]).astype(BF16)
    copies.drain()


def project_kernel(*refs):
    x_a, x_b, out_a, out_b, order = refs[:5]
    grads, (packed, sums, joint, flipped, moved) = refs[5:-5], refs[-5:]
    width = joint.shape[1] // 3
    cols = width // 3
    here = x_a.shape[0]
    flipped[:, pl.ds(0, here)] = x_a[...].T
    flipped[:, pl.ds(here, here)] = x_b[...].T
    for i, grad in enumerate(grads):
        at = pl.ds(i % 3 * width + i // 3 * PAIR, PAIR)
        joint[:, at] = grad[...]
    sums[...] = jnp.sum(joint[...].astype(F32), axis=0, keepdims=True)
    for p in range(3):
        rearrange(order, p, flipped, moved)
        packed[p, :, pl.ds(0, width)] = nn(
            moved[...], joint[:, pl.ds(p * width, width)]
        ).astype(BF16)
        packed[p, :, pl.ds(width, cols)] = (
            out_a[p].astype(F32) + out_b[p].astype(F32)
        ).astype(BF16)


def tokens_kernel(joint, w_query, w_key, w_value, grad_one, part_ref, own_ref):
    rows, width = own_ref.shape[0], w_query.shape[1]
    for first, out_ref in ((rows, part_ref), (0, own_ref)):
        total = grad_one[...] if first == 0 else 0.0
        for i, weight in enumerate((w_query, w_key, w_value)):
            part = joint[pl.ds(first, rows), pl.ds(i * width, width)]
            total = total + nt(part, weight[...])
        out_ref[...] = total.astype(out_ref.dtype)


def unpack_both_kernel(a_ref, b_ref, c_ref, order, down_ref, up_ref, natural):
    size, cols = a_ref.shape[0] // BLOCKS, a_ref.shape[1] // 2
    for p, ref in enumerate((a_ref, b_ref, c_ref)):
        here = pl.ds(p * cols, cols)
        for place in range(BLOCKS):
            rows = pl.ds(pl.multiple_of(order[p, place] * size, 16), size)
            at = pl.ds(place * size, size)
            natural[rows, here] = ref[at, pl.ds(0, cols)].astype(F32)
            up_ref[rows, here] = ref[at, pl.ds(cols, cols)].astype(F32)
        down_ref[here, :] = natural[:, here].T


def unpack_project_kernel(a_ref, b_ref, c_ref, order, q_ref, k_ref, v_ref, out_ref, natural):
    width = q_ref.shape[1]
    size, cols = a_ref.shape[0] // BLOCKS, width // 3
    for p, (ref, grad) in enumerate(((a_ref, q_ref), (b_ref, k_ref), (c_ref, v_ref))):
        for place in range(BLOCKS):
            rows = pl.ds(pl.multiple_of(order[p, place] * size, 16), size)
            grad[rows, :] = ref[pl.ds(place * size, size), pl.ds(0, width)].astype(F32)
            natural[rows, pl.ds(p * cols, cols)] = ref[
                pl.ds(place * size, size), pl.ds(width, cols)
            ].astype(F32)
    out_ref[...] = natural[...].T


def swap(value, bit, count, name="swap"):
    with jax.named_scope(name):
        return lax.ppermute(value, "dp", [(i, i ^ bit) for i in range(count)])


def across(value):
    return lax.ppermute(value, "tensor", [(0, 1), (1, 0)])


def add(left, right):
    return (left.astype(F32) + right.astype(F32)).astype(BF16)


STAGES = ((1, 2, 4, 8), (2, 4, 1, 8), (4, 1, 2, 8))


def block_order():
    mine = lax.rem(lax.axis_index("dp"), BLOCKS // 2)
    rows = []
    for bits in STAGES:
        rows.append(
            [
                sum(bit for i, bit in enumerate(bits) if place >> (len(bits) - 1 - i) & 1)
                for place in range(BLOCKS)
            ]
        )
    return jnp.bitwise_xor(jnp.array(rows, jnp.int32), mine.astype(jnp.int32))


def halves(own, other):
    half = own.shape[1] // 2
    both = [
        [own[p, side * half : (side + 1) * half] for p in range(3)] for side in range(2)
    ]
    if other is not None:
        both = [
            [add(both[side][p], other[p, side * half : (side + 1) * half]) for p in range(3)]
            for side in range(2)
        ]
    return both


def send_stage(sends, step, count, name):
    return [
        swap(sends[p], STAGES[p][step], count, f"{name}_send{step}_{p}") for p in range(3)
    ]


def next_halves(keeps, gots):
    half = keeps[0].shape[0] // 2
    cut = lambda side: [
        add(keeps[p][side * half : (side + 1) * half], gots[p][side * half : (side + 1) * half])
        for p in range(3)
    ]
    return cut(0), cut(1)


def last_stages(keep, got, count, name):
    both = add(keep, got)
    extra = BLOCKS // 2
    while extra < count:
        both = add(both, swap(both, extra, count, name))
        extra *= 2
    return both


def gather_stage(values, step, count, name):
    return [
        jnp.concatenate(
            [values[p], swap(values[p], STAGES[p][step], count, f"{name}_gather{step}_{p}")],
            axis=0,
        )
        for p in range(3)
    ]


def after(values, *earlier):
    return lax.optimization_barrier((values, *earlier))[0]


def shards(
    tokens, segment_ids, w_query, w_key, w_value, b_query, b_value, w_out, b_out, gain_attn,
    shift_attn, w_up, b_up, w_down, b_down, gain_ffn, shift_ffn, cotangent,
):
    count = lax.axis_size("dp")
    here, model = tokens.shape
    width, half = w_query.shape[1], w_up.shape[1]
    row = lambda vector: vector.reshape(1, -1)

    tokens_b = across(tokens)
    segments_b, bu_b = across(segment_ids), across(b_up)
    wo_b, wu_b, wd_b = across(w_out), across(w_up), across(w_down)
    order = block_order()
    one_row = here < LEN
    lay = lambda own, other: (
        [own, other] if one_row else [jnp.concatenate([own, other], axis=0)]
    )
    segs = lay(segment_ids, segments_b)
    query, key, value, contexts, lse = attention_forward(
        lay(tokens, tokens_b), after(segs, order), w_query, w_key, w_value, b_query, b_value
    )
    if one_row:
        ctx_a, ctx_b = contexts
    else:
        ctx_a, ctx_b = contexts[0][:here], contexts[0][here:]
    ctx_b = across(ctx_b)

    low = lambda *dims: shape(*dims, dtype=BF16)
    held = lambda *dims: pltpu.VMEM(dims, BF16)
    wide = lambda *dims: pltpu.VMEM(dims, F32)
    parts = low(3, model, half // 3)
    (
        inverse_one, sums_two, mixed, after_low, normed_one, slope, grad_two, grad_two_low,
        down_b, grad_moved, act_a,
    ) = call(
        forward_kernel,
        [
            shape(here, 1), shape(8, model), low(here, model), low(here, model),
            shape(here, model), low(here, 2 * half), shape(here, model), low(here, model),
            parts, low(3, model, here), low(here, half),
        ],
        [
            tokens, ctx_a, ctx_b, w_out, wo_b, b_out, gain_attn, shift_attn, b_down, gain_ffn,
            shift_ffn, b_up, bu_b, order, w_up, wu_b, w_down, wd_b, cotangent,
        ],
        [
            held(model, 2 * half), held(2 * half, model), held(here, model), held(here, model),
            held(here, model), wide(here, model), held(here, 2 * half), wide(here, model),
            held(here, model), held(here, 2 * half), held(model, here), held(3, model, here),
            held(3, model, half // 3), wide(here, model), pltpu.SemaphoreType.DMA((40,)),
        ],
        limit=56,
        smem=(13,),
        hbm=(14, 15, 16, 17, 18),
        hbm_outs=range(2, 11),
        us=23,
    )
    down_got = across(down_b)

    sums_up, gu, down_a, up_a, up_b = call(
        upper_kernel,
        [shape(1, 2 * half), low(here, 2 * half), parts, parts, parts],
        [order, grad_two_low, after_low, grad_moved, act_a, slope, w_down, wd_b],
        [
            held(2 * half, model), held(here, 2 * half), held(here, 2 * half),
            held(here, model), held(here, model), held(3, model, here), held(here, half),
            held(model, here), held(3, model, here), held(3, 3, model, half // 3),
            pltpu.SemaphoreType.DMA((40,)),
        ],
        smem=(0,),
        hbm=(1, 2, 3, 4, 5, 6, 7),
        hbm_outs=(1, 2, 3, 4),
        limit=60,
        us=12,
    )
    up_got = across(up_b)
    down_keep, down_send = halves(down_a, down_got)
    down_new = send_stage(down_send, 0, count, "down")
    up_keep, up_send = halves(after(up_a, down_send), up_got)
    up_new = send_stage(up_send, 0, count, "up")

    sums_one, gctx_a, gctx_b, out_a, out_b, grad_one = call(
        first_norm_kernel,
        [
            shape(8, model), low(here, width), low(here, width),
            low(3, model, width // 3), low(3, model, width // 3), shape(here, model),
        ],
        [
            inverse_one, gain_attn, order, w_out, wo_b, ctx_a, ctx_b, grad_two, normed_one,
            after(gu, down_send, up_send), w_up, wu_b,
        ],
        [
            held(here, 2 * half), held(model, 2 * half), wide(here, model), wide(here, model),
            wide(here, model), wide(here, model), held(here, model), held(model, here),
            held(model, here), pltpu.SemaphoreType.DMA((24,)),
        ],
        smem=(2,),
        hbm=(7, 8, 9, 10, 11),
        hbm_outs=(5,),
        us=12,
    )
    grad_contexts = lay(gctx_a, across(gctx_b))
    out_got = across(out_b)

    back = lambda pair, earlier: attention_backward(
        pair, query, key, value, contexts, after(grad_contexts, earlier), lse, segs
    )
    join = lambda one, two: [jnp.concatenate(pair, axis=1) for pair in zip(one, two)]
    down_keep, down_send = next_halves(down_keep, after(down_new, sums_one))
    up_keep, up_send = next_halves(up_keep, after(up_new, sums_one))
    both_keep, both_send = join(down_keep, up_keep), join(down_send, up_send)
    both_new = send_stage(both_send, 1, count, "both")
    grads = back(0, both_send)
    both_keep, both_send = next_halves(both_keep, after(both_new, grads))
    both_new = send_stage(both_send, 2, count, "both")
    grads += back(1, (grads, both_send))
    both_keep, both_new = after((both_keep, both_new), grads)
    exchange = lambda p: last_stages(both_keep[p], both_new[p], count, f"both_exchange{p}")
    both = [exchange(0)]
    grads += back(2, (grads, both_new))
    both_keep, both_new = after((both_keep, both_new), both, grads)
    both.append(exchange(1))

    packed, sums_three, joint = call(
        project_kernel,
        [parts, shape(1, 3 * width), low(2 * here, 3 * width)],
        [tokens, tokens_b, out_a, out_got, order, *after(grads, both[0])],
        [held(model, 2 * here), held(model, 2 * here)],
        smem=(4,),
        us=7,
    )
    last_keep, last_send = halves(packed, None)
    last_new = send_stage(last_send, 0, count, "last")
    both_keep, both_new = after((both_keep, both_new), both, last_send)
    both.append(exchange(2))
    token_part, token_own = call(
        tokens_kernel,
        [low(here, model), shape(here, model)],
        [after(joint, last_send, both[1]), w_query, w_key, w_value, grad_one],
        us=5,
    )
    token_got = across(token_part)
    grad_tokens = token_own + token_got.astype(F32)

    shared = jnp.concatenate([sums_one[:3], sums_two[:3]], axis=0)
    shared, sums_up = after((shared, sums_up), token_own)
    sums_up = sums_up[0, :half] + across(sums_up[0, half:])
    shared = (shared + across(shared)).reshape(-1)
    small = jnp.concatenate(
        [shared, sums_three[0, :width], sums_three[0, 2 * width :], sums_up]
    ).reshape(-1, 128)
    bits = [1 << i for i in range(count.bit_length() - 1)]
    step_small = lambda value, i: value + swap(value, bits[i], count, f"small{i}")

    last_keep, last_send = next_halves(last_keep, after(last_new, token_own))
    last_new = send_stage(last_send, 1, count, "last")
    both = gather_stage(after(both, last_send), 2, count, "both")
    small = step_small(after(small, last_send), 0)
    last_keep, last_send = next_halves(last_keep, after(last_new, both))
    last_new = send_stage(last_send, 2, count, "last")
    both = gather_stage(after(both, last_send), 1, count, "both")
    small = step_small(after(small, last_send), 1)
    last_keep, last_new = after((last_keep, last_new), small)
    last = jnp.split(
        last_stages(
            jnp.concatenate(last_keep), jnp.concatenate(last_new), count, "last_exchange"
        ),
        3,
    )
    both = gather_stage(both, 0, count, "both")
    small = step_small(small, 2)
    last = gather_stage(after(last, small), 2, count, "last")
    last = gather_stage(after(last, both), 1, count, "last")
    for i in range(3, len(bits)):
        small = step_small(after(small, last), i)
    last = gather_stage(last, 0, count, "last")
    grad_w_down, grad_w_up = call(
        unpack_both_kernel,
        [shape(half, model), shape(model, half)],
        [*both, order],
        [wide(model, half)],
        limit=40,
        smem=(3,),
    )
    grad_w_query, grad_w_key, grad_w_value, grad_w_out = call(
        unpack_project_kernel,
        [shape(model, width)] * 3 + [shape(width, model)],
        [*last, order],
        [wide(model, width)],
        limit=40,
        smem=(3,),
    )

    small = small.reshape(-1)
    cuts = [model * i for i in range(1, 7)] + [6 * model + width, 6 * model + 2 * width]
    (
        grad_gain_attn, grad_shift_attn, grad_b_out, grad_gain_ffn, grad_shift_ffn, grad_b_down,
        grad_b_query, grad_b_value, grad_b_up,
    ) = jnp.split(small, cuts)
    return (
        mixed, grad_tokens, grad_w_query, grad_w_key, grad_w_value, grad_b_query, grad_b_value,
        grad_w_out, grad_b_out, grad_gain_attn, grad_shift_attn, grad_w_up, grad_b_up, grad_w_down,
        grad_b_down, grad_gain_ffn, grad_shift_ffn,
    )


def solution(mesh):
    placed = (
        P(("dp", "tensor"), None),
        P(("dp", "tensor")),
        P(None, "tensor"),
        P(None, "tensor"),
        P(None, "tensor"),
        P("tensor"),
        P("tensor"),
        P("tensor", None),
        P(),
        P(),
        P(),
        P(None, "tensor"),
        P("tensor"),
        P("tensor", None),
        P(),
        P(),
        P(),
        P(("dp", "tensor"), None),
    )
    return jax.shard_map(
        shards,
        mesh=mesh,
        in_specs=placed,
        out_specs=(
            P(("dp", "tensor"), None),
            P(("dp", "tensor"), None),
            P(None, "tensor"),
            P(None, "tensor"),
            P(None, "tensor"),
            P("tensor"),
            P("tensor"),
            P("tensor", None),
            P(),
            P(),
            P(),
            P(None, "tensor"),
            P("tensor"),
            P("tensor", None),
            P(),
            P(),
            P(),
        ),
        check_vma=False,
    )
```

```python
from functools import partial

import jax
import jax.numpy as jnp
from jax import lax
from jax.experimental import pallas as pl
from jax.experimental.pallas import tpu as pltpu
from jax.sharding import PartitionSpec as P

HD = 64
LEN = 1024
EPSILON = 1e-05
MASKED = -1e30
SCALE = HD**-0.5
BLOCKS = 16
PAIR = 2 * HD
MIB = 1 << 20

F32 = jnp.float32
BF16 = jnp.bfloat16


def nn(left, right):
    return lax.dot_general(left, right, (((1,), (0,)), ((), ())), preferred_element_type=F32)


def nt(left, right):
    return lax.dot_general(left, right, (((1,), (1,)), ((), ())), preferred_element_type=F32)


def tn(left, right):
    return lax.dot_general(left, right, (((0,), (0,)), ((), ())), preferred_element_type=F32)


def normalize_parts(hidden):
    average = jnp.mean(hidden, axis=-1, keepdims=True)
    centred = hidden - average
    spread = jnp.mean(centred * centred, axis=-1, keepdims=True)
    inverse = lax.rsqrt(spread + EPSILON)
    return centred * inverse, inverse


def normalize_back(grad_out, normed, inverse, gain):
    scaled = grad_out * gain
    first_mean = jnp.mean(scaled, axis=-1, keepdims=True)
    second_mean = jnp.mean(scaled * normed, axis=-1, keepdims=True)
    return inverse * (scaled - first_mean - normed * second_mean)


def gelu_parts(upper):
    phi = 0.5 + 0.5 * lax.erf(upper * 0.5**0.5)
    bell = jnp.exp(upper * upper * -0.5)
    return upper * phi, phi + upper * bell * 0.3989422804014327


def lasting(us):
    return pl.CostEstimate(flops=int(us * 1.15e9), bytes_accessed=0, transcendentals=0)


def call(kernel, outs, ins, scratch=(), limit=48, smem=(), hbm=(), hbm_outs=(), us=5):
    place = lambda i, far: pl.BlockSpec(memory_space=pl.ANY if i in far else pltpu.VMEM)
    return pl.pallas_call(
        kernel,
        out_shape=outs,
        in_specs=[
            pl.BlockSpec(memory_space=pltpu.SMEM) if i in smem else place(i, hbm)
            for i in range(len(ins))
        ],
        out_specs=[place(i, hbm_outs) for i in range(len(outs))],
        scratch_shapes=list(scratch),
        compiler_params=pltpu.CompilerParams(vmem_limit_bytes=limit * MIB),
        cost_estimate=lasting(us),
    )(*ins)


def shape(*dims, dtype=F32):
    return jax.ShapeDtypeStruct(dims, dtype)


def as_row(ref):
    return ref[...].reshape(1, -1)


def join_segments(refs):
    return jnp.concatenate([as_row(ref).astype(F32) for ref in refs], axis=1)


def as_column(row):
    return jnp.broadcast_to(row, (8, row.shape[1])).T[:, :1]


def pairs(heads):
    return [pl.ds(pair * PAIR, PAIR) for pair in range(heads // 2)]


def split_pair(block):
    owner = lax.broadcasted_iota(jnp.int32, block.shape, 1) // HD
    empty = jnp.zeros_like(block)
    return jnp.concatenate(
        [jnp.where(owner == 0, block, empty), jnp.where(owner == 1, block, empty)], axis=0
    )


def attend_kernel(*refs, split):
    xs, refs = refs[:split], refs[split:]
    segs, refs = refs[:split], refs[split:]
    wq_ref, wk_ref, wv_ref, bq_ref, bv_ref = refs[:5]
    q_ref, k_ref, v_ref, *ctx_refs, lse_ref, bias, vt, ctxt = refs[5:]
    heads = q_ref.shape[1] // HD
    block = 256
    segments = join_segments(segs)
    bias[...] = jnp.where(as_column(segments) == segments, 0.0, MASKED)
    size = LEN // split
    for i, x_ref in enumerate(xs):
        x, rows = x_ref[...], pl.ds(i * size, size)
        q_ref[rows, :] = ((nn(x, wq_ref[...]) + as_row(bq_ref)) * SCALE).astype(BF16)
        k_ref[rows, :] = nn(x, wk_ref[...]).astype(BF16)
        value = (nn(x, wv_ref[...]) + as_row(bv_ref)).astype(BF16)
        v_ref[rows, :] = value
        vt[:, rows] = value.T

    @pl.loop(0, LEN // block)
    def _(j):
        here = pl.ds(pl.multiple_of(j * block, block), block)
        products = [
            nt(k_ref[:, lanes], split_pair(q_ref[here, lanes])) for lanes in pairs(heads)
        ]
        mask = bias[:, here]
        weights, tops, totals = [], [], []
        for head in range(heads):
            start = head % 2 * block
            scores = products[head // 2][:, start : start + block] + mask
            tops.append(jnp.max(scores, axis=0, keepdims=True))
            weight = jnp.exp(scores - tops[-1])
            totals.append(jnp.sum(weight, axis=0, keepdims=True))
            weights.append(weight.astype(BF16))
        for head in range(heads):
            at = pl.ds(head * HD, HD)
            ctxt[at, here] = nn(vt[at, :], weights[head]) * (1.0 / totals[head])
            lse_ref[0, pl.ds(head, 1), here] = tops[head] + jnp.log(totals[head])

    for i, ctx_ref in enumerate(ctx_refs):
        ctx_ref[...] = ctxt[:, pl.ds(i * size, size)].T.astype(BF16)


def attention_forward(xs, segs, w_query, w_key, w_value, b_query, b_value):
    split = len(xs)
    size = LEN // split
    rows, model = xs[0].shape[0] // size, xs[0].shape[1]
    width = w_query.shape[1]
    by_row = pl.BlockSpec((LEN, width), lambda r: (r, 0))
    by_part = pl.BlockSpec((size, width), lambda r: (r, 0))
    whole = lambda *dims: pl.BlockSpec(dims, lambda r: (0,) * len(dims))
    us = 13 * rows
    query, key, value, *contexts, lse = pl.pallas_call(
        partial(attend_kernel, split=split),
        grid=(rows,),
        out_shape=[shape(rows * LEN, width, dtype=BF16)] * 3
        + [shape(rows * size, width, dtype=BF16)] * split
        + [shape(rows, 8, LEN)],
        in_specs=[pl.BlockSpec((size, model), lambda r: (r, 0))] * split
        + [pl.BlockSpec((size,), lambda r: (r,))] * split
        + [
            whole(model, width),
            whole(model, width),
            whole(model, width),
            whole(width),
            whole(width),
        ],
        out_specs=[by_row] * 3
        + [by_part] * split
        + [pl.BlockSpec((1, 8, LEN), lambda r: (r, 0, 0))],
        scratch_shapes=[
            pltpu.VMEM((LEN, LEN), F32),
            pltpu.VMEM((width, LEN), BF16),
            pltpu.VMEM((width, LEN), F32),
        ],
        compiler_params=pltpu.CompilerParams(vmem_limit_bytes=60 * MIB),
        cost_estimate=lasting(us),
    )(*xs, *segs, w_query, w_key, w_value, b_query, b_value)
    return query, key, value, contexts, lse


def attend_back_kernel(
    q_ref, k_ref, v_ref, lse_ref, *refs, pair, split
):
    segs, ctx_refs, dctx_refs = (refs[i * split : (i + 1) * split] for i in range(3))
    dq_ref, dk_ref, dv_ref, kt, dqt, dk_sum, dv_sum, inner, dctx_ref, ctx_ref, seg = refs[
        3 * split :
    ]
    size = LEN // split
    for i in range(split):
        dctx_ref[pl.ds(i * size, size), :] = dctx_refs[i][...]
        ctx_ref[pl.ds(i * size, size), :] = ctx_refs[i][...]
    width = q_ref.shape[1]
    block = 256
    kt[...] = k_ref[...].T
    seg[...] = join_segments(segs)
    column = as_column(seg[...])
    picks = lax.broadcasted_iota(jnp.int32, (8, width), 0) == (
        lax.broadcasted_iota(jnp.int32, (8, width), 1) // HD
    )
    product = ctx_ref[...].astype(F32) * dctx_ref[...].astype(F32)
    inner[...] = lax.dot_general(
        picks.astype(F32), product, (((1,), (1,)), ((), ())),
        precision=lax.Precision.HIGHEST, preferred_element_type=F32,
    )
    dk_sum[...] = jnp.zeros_like(dk_sum)
    dv_sum[...] = jnp.zeros_like(dv_sum)

    @pl.loop(0, LEN // block)
    def _(j):
        here = pl.ds(pl.multiple_of(j * block, block), block)
        allowed = column == seg[:, here]
        queries, grads = split_pair(q_ref[here, :]), split_pair(dctx_ref[here, :])
        products, slopes = nt(k_ref[...], queries), nt(v_ref[...], grads)
        weights, changes = [], []
        for side in range(2):
            at = slice(side * block, (side + 1) * block)
            scores = jnp.where(allowed, products[:, at], MASKED)
            weight = jnp.exp(scores - lse_ref[0, 2 * pair + side : 2 * pair + side + 1, here])
            change = weight * (slopes[:, at] - inner[side : side + 1, here])
            weights.append(weight.astype(BF16))
            changes.append(change.astype(BF16))
        dv_sum[...] += nn(jnp.concatenate(weights, axis=1), grads)
        dk_sum[...] += nn(jnp.concatenate(changes, axis=1), queries)
        for side in range(2):
            at = slice(side * HD, (side + 1) * HD)
            dqt[at, here] = nn(kt[at, :], changes[side]) * SCALE

    dq_ref[...] = dqt[...].T.astype(BF16)
    dk_ref[...] = dk_sum[...].astype(BF16)
    dv_ref[...] = dv_sum[...].astype(BF16)


def attention_backward(pair, query, key, value, contexts, grads, lse, segs):
    rows, split = query.shape[0] // LEN, len(contexts)
    columns = pl.BlockSpec((LEN, PAIR), lambda r: (r, pair))
    part = pl.BlockSpec((LEN // split, PAIR), lambda r: (r, pair))
    own = pl.BlockSpec((LEN, PAIR), lambda r: (r, 0))
    us = 7 * rows
    return pl.pallas_call(
        partial(attend_back_kernel, pair=pair, split=split),
        grid=(rows,),
        out_shape=[shape(rows * LEN, PAIR, dtype=BF16)] * 3,
        in_specs=[columns] * 3
        + [
            pl.BlockSpec((1, 8, LEN), lambda r: (r, 0, 0)),
        ]
        + [pl.BlockSpec((LEN // split,), lambda r: (r,))] * split
        + [part] * (2 * split),
        out_specs=[own] * 3,
        scratch_shapes=[
            pltpu.VMEM((PAIR, LEN), BF16),
            pltpu.VMEM((PAIR, LEN), F32),
            pltpu.VMEM((LEN, PAIR), F32),
            pltpu.VMEM((LEN, PAIR), F32),
            pltpu.VMEM((8, LEN), F32),
            pltpu.VMEM((LEN, PAIR), BF16),
            pltpu.VMEM((LEN, PAIR), BF16),
            pltpu.VMEM((1, LEN), F32),
        ],
        compiler_params=pltpu.CompilerParams(vmem_limit_bytes=24 * MIB),
        cost_estimate=lasting(us),
    )(query, key, value, lse, *segs, *contexts, *grads)


def rearrange(order, source, target):
    third = source.shape[0] // 3
    size = third // BLOCKS
    for p in range(3):
        for place in range(BLOCKS):
            rows = pl.ds(pl.multiple_of(p * third + order[p, place] * size, 16), size)
            target[pl.ds(p * third + place * size, size), :] = source[rows, :]


class Copies:
    def __init__(self, sems):
        self.sems, self.used, self.open = sems, 0, []

    def start(self, source, target):
        copy = pltpu.make_async_copy(source, target, self.sems.at[self.used])
        self.used += 1
        copy.start()
        return copy

    def store(self, source, target):
        self.open.append(self.start(source, target))

    def drain(self):
        for copy in self.open:
            copy.wait()


def as_lines(row, cols):
    return jnp.concatenate(
        [row[:, i : i + cols] for i in range(0, row.shape[1], cols)], axis=0
    )


def split_small(values):
    high = values.astype(BF16)
    return jnp.concatenate([high, (values - high.astype(F32)).astype(BF16)], axis=0)


def layer_kernel(
    x_ref, ctx_a, ctx_b, wo_a, wo_b, b_out, gain_one, shift_one, b_down, gain_two, shift_two,
    bu_a, bu_b, order, wu_a, wu_b, wd_a, wd_b, cot_hbm,
    sums_ref, gctx_a, gctx_b, out_a, out_b, mixed_hbm, one_hbm, down_a, down_b, up_a, up_b,
    wu, wd, cot, mixed, after_buf, normed_buf, inverse_buf, slope, grad_buf, low_buf, act,
    flipped, moved, parts, total, sems,
):
    rows, model = x_ref.shape
    half = wu_a.shape[1]
    chunk = 512
    copies = Copies(sems)
    ups, downs = [], []
    for side, up in enumerate((wu_a, wu_b)):
        for start in range(0, half, chunk):
            to = pl.ds(side * half + start, chunk)
            ups.append(copies.start(up.at[:, pl.ds(start, chunk)], wu.at[:, to]))
    for side, down in enumerate((wd_a, wd_b)):
        downs.append(copies.start(down, wd.at[pl.ds(side * half, half), :]))
    cot_copy = copies.start(cot_hbm, cot)
    b_out, gain_one, shift_one, b_down, gain_two, shift_two = map(
        as_row, (b_out, gain_one, shift_one, b_down, gain_two, shift_two)
    )
    biases = [as_row(bu_a), as_row(bu_b)]

    hidden = nn(ctx_a[...], wo_a[...]) + nn(ctx_b[...], wo_b[...])
    normed, inverse = normalize_parts(x_ref[...].astype(F32) + hidden + b_out)
    normed_buf[...] = normed
    inverse_buf[...] = inverse
    after_buf[...] = (normed * gain_one + shift_one).astype(BF16)

    def raise_up(i):
        ups[i].wait()
        here = pl.ds(i * chunk, chunk)
        start = i * chunk % half
        bias = biases[i * chunk // half][:, start : start + chunk]
        return nn(after_buf[...], wu[:, here]) + bias

    count = 2 * half // chunk
    upper = raise_up(0)
    for i in range(count):
        following = raise_up(i + 1) if i + 1 < count else None
        here = pl.ds(i * chunk, chunk)
        active, steep = gelu_parts(upper)
        act[:, here] = active.astype(BF16)
        slope[:, here] = steep.astype(BF16)
        upper = following
    for copy in downs:
        copy.wait()
    total[...] = nn(act[...], wd[...])
    cot_copy.wait()

    after = normed_buf[...] * gain_one + shift_one
    normed, inverse = normalize_parts(after + total[...] + b_down)
    mixed[...] = (normed * gain_two + shift_two).astype(BF16)
    copies.store(mixed, mixed_hbm)
    outer = cot[...].astype(F32)
    grad = normalize_back(outer, normed, inverse, gain_two)
    grad_buf[...] = grad
    low_buf[...] = grad.astype(BF16)
    add_up = lambda values: jnp.sum(values, axis=0, keepdims=True)
    sums_two = [add_up(outer * normed), add_up(outer), add_up(grad)]

    flipped[...] = grad_buf[...].T.astype(BF16)
    rearrange(order, flipped, moved)
    for side, out in ((1, down_b), (0, down_a)):
        parts[side] = nn(moved[...], act[:, pl.ds(side * half, half)]).astype(BF16)
        copies.store(parts.at[side], out)
    flipped[...] = after_buf[...].T
    rearrange(order, flipped, moved)
    sums_up = [None, None]
    for side, out in ((1, up_b), (0, up_a)):
        here = pl.ds(side * half, half)
        pulled = nt(low_buf[...], wd[here, :])
        slope[:, here] = (pulled * slope[:, here].astype(F32)).astype(BF16)
        sums_up[side] = add_up(slope[:, here].astype(F32))
        parts[2 + side] = nn(moved[...], slope[:, here]).astype(BF16)
        copies.store(parts.at[2 + side], out)
    total[...] = nt(slope[...], wu[...])

    after = grad_buf[...] + total[...]
    normed = normed_buf[...]
    grad = normalize_back(after, normed, inverse_buf[...], gain_one)
    grad_buf[...] = grad
    copies.store(grad_buf, one_hbm)
    low_buf[...] = grad.astype(BF16)
    gctx_b[...] = nt(low_buf[...], wo_b[...]).astype(BF16)
    gctx_a[...] = nt(low_buf[...], wo_a[...]).astype(BF16)
    flipped[...] = grad_buf[...].T.astype(BF16)
    rearrange(order, flipped, moved)
    out_b[pl.ds(0, model), :] = nn(moved[...], ctx_b[...]).astype(BF16)
    out_a[...] = nn(moved[...], ctx_a[...]).astype(BF16)

    cols = ctx_a.shape[1] // 3
    sums = [add_up(after * normed), add_up(after), add_up(grad), *sums_two]
    shared = as_lines(jnp.concatenate(sums, axis=1), cols)
    own, other = (as_lines(part, cols) for part in sums_up)
    sums_ref[...] = jnp.concatenate([shared, own], axis=0)
    rider = split_small(jnp.concatenate([shared, other], axis=0))
    lines = rider.shape[0] // 3
    for i in range(3):
        out_b[pl.ds(model, lines), pl.ds(i * cols, cols)] = rider[i * lines : (i + 1) * lines]
    copies.drain()


SMALL = 16


def project_kernel(*refs):
    x_a, x_b, out_a, out_b, sums_ref, order = refs[:6]
    grads, outs = refs[6:15], refs[15:]
    keeps, sends, (small, joint, flipped, moved) = outs[:3], outs[3:6], outs[6:]
    width = joint.shape[1] // 3
    cols = width // 3
    here, model = x_a.shape
    half = keeps[0].shape[0]
    flipped[:, pl.ds(0, here)] = x_a[...].T
    flipped[:, pl.ds(here, here)] = x_b[...].T
    for i, grad in enumerate(grads):
        at = pl.ds(i % 3 * width + i // 3 * PAIR, PAIR)
        joint[:, at] = grad[...]
    rearrange(order, flipped, moved)
    product = nn(moved[...], joint[...]).astype(BF16)
    other = (out_a[...].astype(F32) + out_b[pl.ds(0, model), :].astype(F32)).astype(BF16)
    for p in range(3):
        for i, out in enumerate((keeps[p], sends[p])):
            rows = slice((2 * p + i) * half, (2 * p + i + 1) * half)
            out[pl.ds(0, half), pl.ds(0, 3 * width)] = product[rows]
            out[pl.ds(0, half), pl.ds(3 * width, width)] = other[rows]
    sums = jnp.sum(joint[...].astype(F32), axis=0, keepdims=True)
    lines = out_b.shape[0] - model
    rider = [out_b[pl.ds(model, lines), pl.ds(i * cols, cols)] for i in range(3)]
    rider = jnp.concatenate(rider, axis=0).astype(F32)
    count = sums_ref.shape[0]
    shared = sums_ref[...] + (rider[:count] + rider[count:])
    per = small.shape[1] // cols
    small[...] = jnp.zeros_like(small)
    for i in range(count):
        small[pl.ds(i // per, 1), pl.ds(i % per * cols, cols)] = shared[i : i + 1]
    rows = count // per
    small[pl.ds(rows, 1), pl.ds(0, width)] = sums[:, :width]
    small[pl.ds(rows + 1, 1), pl.ds(0, width)] = sums[:, 2 * width :]
    sends[0][pl.ds(half, SMALL), :] = jnp.zeros((SMALL, sends[0].shape[1]), BF16)
    high = split_small(small[...])
    for i in range(2):
        sends[0][pl.ds(half, SMALL), pl.ds(i * small.shape[1], small.shape[1])] = high[
            i * SMALL : (i + 1) * SMALL
        ]


def tokens_kernel(joint, w_query, w_key, w_value, grad_one, part_ref, own_ref):
    rows, width = own_ref.shape[0], w_query.shape[1]
    for first, out_ref in ((rows, part_ref), (0, own_ref)):
        total = grad_one[...] if first == 0 else 0.0
        for i, weight in enumerate((w_query, w_key, w_value)):
            part = joint[pl.ds(first, rows), pl.ds(i * width, width)]
            total = total + nt(part, weight[...])
        out_ref[...] = total.astype(out_ref.dtype)


def unpack(order, lows, highs, put):
    third = 2 * lows[0].shape[0]
    size = third // BLOCKS
    for p, halves_of_part in enumerate(zip(lows, highs)):
        for place in range(BLOCKS):
            rows = pl.ds(pl.multiple_of(p * third + order[p, place] * size, 8), size)
            side, at = divmod(place, BLOCKS // 2)
            put(rows, halves_of_part[side][pl.ds(at * size, size), :].astype(F32))


def unpack_both_kernel(*refs):
    lows, highs, (order, down_ref, up_ref, natural) = refs[:3], refs[3:6], refs[6:]
    half = up_ref.shape[1]

    def put(rows, values):
        natural[rows, :] = values[:, :half]
        up_ref[rows, :] = values[:, half:]

    unpack(order, lows, highs, put)
    step = 512
    for start in range(0, half, step):
        here = pl.ds(start, step)
        down_ref[here, :] = natural[:, here].T


def unpack_project_kernel(*refs):
    lows, highs, refs = refs[:3], refs[3:6], refs[6:]
    order, q_ref, k_ref, v_ref, out_ref, natural = refs
    width = q_ref.shape[1]

    def put(rows, values):
        for i, ref in enumerate((q_ref, k_ref, v_ref, natural)):
            ref[rows, :] = values[:, i * width : (i + 1) * width]

    unpack(order, lows, highs, put)
    out_ref[...] = natural[...].T


def swap(value, bit, count, name="swap"):
    with jax.named_scope(name):
        return lax.ppermute(value, "dp", [(i, i ^ bit) for i in range(count)])


def across(value):
    return lax.ppermute(value, "tensor", [(0, 1), (1, 0)])


def add(left, right):
    return (left.astype(F32) + right.astype(F32)).astype(BF16)


STAGES = ((1, 2, 4, 8), (2, 4, 1, 8), (4, 1, 2, 8))


def block_order():
    mine = lax.rem(lax.axis_index("dp"), BLOCKS // 2)
    rows = []
    for bits in STAGES:
        rows.append(
            [
                sum(bit for i, bit in enumerate(bits) if place >> (len(bits) - 1 - i) & 1)
                for place in range(BLOCKS)
            ]
        )
    return jnp.bitwise_xor(jnp.array(rows, jnp.int32), mine.astype(jnp.int32))


def halves(own, other):
    half = own.shape[0] // 6
    cut = lambda at: add(own[at * half : (at + 1) * half], other[at * half : (at + 1) * half])
    return [cut(2 * p) for p in range(3)], [cut(2 * p + 1) for p in range(3)]


def send_stage(sends, step, count, name):
    return [
        swap(sends[p], STAGES[p][step], count, f"{name}_send{step}_{p}") for p in range(3)
    ]


def next_halves(keeps, gots):
    half = keeps[0].shape[0] // 2
    cut = lambda side: [
        add(keeps[p][side * half : (side + 1) * half], gots[p][side * half : (side + 1) * half])
        for p in range(3)
    ]
    return cut(0), cut(1)


def with_rider(rows, small):
    high = split_small(small)
    rider = jnp.concatenate([high[:SMALL], high[SMALL:]], axis=1)
    rider = jnp.pad(rider, ((0, 0), (0, rows.shape[1] - rider.shape[1])))
    return jnp.concatenate([rows, rider], axis=0)


def take_small(got, rows, small):
    rider, width = got[rows:].astype(F32), small.shape[1]
    return got[:rows], small + (rider[:, :width] + rider[:, width : 2 * width])


def halves_and_small(keeps, gots, small):
    first, small = take_small(gots[0], keeps[0].shape[0], small)
    keeps, sends = next_halves(keeps, [first, *gots[1:]])
    return keeps, [with_rider(sends[0], small), *sends[1:]], small


def gather_stage(values, step, count, name):
    return [
        swap(values[p], STAGES[p][step], count, f"{name}_gather{step}_{p}") for p in range(3)
    ]


def after(values, *earlier):
    return lax.optimization_barrier((values, *earlier))[0]


def shards(
    tokens, segment_ids, w_query, w_key, w_value, b_query, b_value, w_out, b_out, gain_attn,
    shift_attn, w_up, b_up, w_down, b_down, gain_ffn, shift_ffn, cotangent,
):
    count = lax.axis_size("dp")
    here, model = tokens.shape
    width, half = w_query.shape[1], w_up.shape[1]
    row = lambda vector: vector.reshape(1, -1)

    tokens_b = across(tokens)
    segments_b, bu_b = across(segment_ids), across(b_up)
    wo_b, wu_b, wd_b = map(across, after((w_out, w_up, w_down), tokens_b))
    order = block_order()
    one_row = here < LEN
    lay = lambda own, other: (
        [own, other] if one_row else [jnp.concatenate([own, other], axis=0)]
    )
    segs = lay(segment_ids, segments_b)
    query, key, value, contexts, lse = attention_forward(
        lay(tokens, tokens_b), after(segs, order), w_query, w_key, w_value, b_query, b_value
    )
    if one_row:
        ctx_a, ctx_b = contexts
    else:
        ctx_a, ctx_b = contexts[0][:here], contexts[0][here:]
    ctx_b = across(ctx_b)

    low = lambda *dims: shape(*dims, dtype=BF16)
    held = lambda *dims: pltpu.VMEM(dims, BF16)
    wide = lambda *dims: pltpu.VMEM(dims, F32)
    lines = (6 * model + half) // (width // 3)
    size = min(here, LEN // 2)

    def layer(at):
        cut = lambda value: value[at : at + size]
        return call(
            layer_kernel,
            [
                shape(lines, width // 3), low(size, width), low(size, width), low(model, width),
                low(model + 2 * lines // 3, width), low(size, model), shape(size, model),
            ] + [low(model, half)] * 4,
            [
                cut(tokens), cut(ctx_a), cut(ctx_b), w_out, wo_b, b_out, gain_attn, shift_attn,
                b_down, gain_ffn, shift_ffn, b_up, bu_b, order, w_up, wu_b, w_down, wd_b,
                cut(cotangent),
            ],
            [
                held(model, 2 * half), held(2 * half, model), held(size, model), held(size, model),
                held(size, model), wide(size, model), wide(size, 1), held(size, 2 * half),
                wide(size, model), held(size, model), held(size, 2 * half), held(model, size),
                held(model, size), held(4, model, half), wide(size, model),
                pltpu.SemaphoreType.DMA((20,)),
            ],
            limit=60,
            smem=(13,),
            hbm=(14, 15, 16, 17, 18),
            hbm_outs=range(5, 11),
            us=35,
        )

    blocks = [layer(at) for at in range(0, here, size)]
    if len(blocks) == 1:
        small_sums, gctx_a, gctx_b, out_a, out_b, mixed, grad_one, *weights = blocks[0]
    else:
        small_sums, gctx_a, gctx_b, out_a, out_b, mixed, grad_one, *weights = (
            jnp.concatenate(each, axis=0)
            if i in (1, 2, 5, 6)
            else sum(part.astype(F32) for part in each).astype(each[0].dtype)
            for i, each in enumerate(zip(*blocks))
        )
    down_a, down_b, up_a, up_b = weights
    grad_contexts = lay(gctx_a, across(gctx_b))
    down_b, up_b, out_b = after((down_b, up_b, out_b), grad_contexts)
    down_got, up_got, out_got = across(down_b), across(up_b), across(out_b)

    back = lambda pair, earlier: attention_backward(
        pair, query, key, value, contexts, after(grad_contexts, earlier), lse, segs
    )
    grads = back(0, grad_contexts)
    down_got, up_got = after((down_got, up_got), grads)
    down_keep, down_send = halves(down_a, down_got)
    up_keep, up_send = halves(up_a, up_got)
    join = lambda one, two: [jnp.concatenate(pair, axis=1) for pair in zip(one, two)]
    both_keep, both_send = join(down_keep, up_keep), join(down_send, up_send)
    both_new = send_stage(both_send, 0, count, "both")

    grads += back(1, (grads, both_send))
    grads += back(2, grads)
    both_keep, both_send = next_halves(both_keep, after(both_new, grads))
    both_new = send_stage(both_send, 1, count, "both")
    grads = after(grads, both_send)
    sixth = low(model // 6, 4 * width)
    *last, small, joint = call(
        project_kernel,
        [sixth] * 3
        + [low(model // 6 + SMALL, 4 * width), sixth, sixth]
        + [shape(SMALL, half // 3), low(2 * here, 3 * width)],
        [
            tokens, tokens_b, out_a, out_got, small_sums, order, *grads,
        ],
        [held(model, 2 * here), held(model, 2 * here)],
        smem=(5,),
        us=7,
    )
    last_keep, last_send = last[:3], last[3:]
    both_keep, both_send = next_halves(both_keep, after(both_new, last))
    both_new = send_stage(both_send, 2, count, "both")
    last_send = after(last_send, both_send)
    last_new = send_stage(last_send, 0, count, "last")
    token_part, token_own = call(
        tokens_kernel,
        [low(here, model), shape(here, model)],
        [after(joint, last_send), w_query, w_key, w_value, grad_one],
        us=5,
    )
    token_got = across(token_part)

    join_rows = lambda one, two: [jnp.concatenate(pair, axis=0) for pair in zip(one, two)]
    meet = lambda keeps, gots: jnp.concatenate([add(k, g) for k, g in zip(keeps, gots)], axis=0)
    apart = lambda value: [
        value[i * value.shape[0] // 3 : (i + 1) * value.shape[0] // 3] for i in range(3)
    ]
    extras = [BLOCKS // 2 << i for i in range((count // (BLOCKS // 2)).bit_length() - 1)]
    both_value = meet(both_keep, after(both_new, token_own))
    both_got = swap(both_value, extras[0], count, "both_exchange")

    last_keep, last_send, small = halves_and_small(last_keep, after(last_new, both_value), small)
    last_new = send_stage(last_send, 1, count, "last")
    last_keep, last_send, small = halves_and_small(last_keep, last_new, small)
    last_new = send_stage(last_send, 2, count, "last")
    grad_tokens = token_own + after(token_got, last_send).astype(F32)
    first, small = take_small(last_new[0], last_keep[0].shape[0], small)
    last_value = meet(last_keep, [first, *last_new[1:]])
    rider = with_rider(last_value, small)
    last_got = swap(rider, extras[0], count, "last_exchange")

    both_value = add(both_value, after(both_got, rider))
    for extra in extras[1:]:
        both_value = add(both_value, swap(both_value, extra, count))
    both = apart(both_value)
    both = join_rows(both, gather_stage(both, 2, count, "both"))
    both_new = gather_stage(both, 1, count, "both")

    last_got, small = take_small(after(last_got, both), last_value.shape[0], small)
    last_value = add(last_value, last_got)
    for extra in extras[1:]:
        got = swap(with_rider(last_value, small), extra, count)
        got, small = take_small(got, last_value.shape[0], small)
        last_value = add(last_value, got)
    last = apart(last_value)
    last_new = gather_stage(last, 2, count, "last")
    both = join_rows(both, after(both_new, last))
    last = join_rows(last, after(last_new, both))
    last_new = gather_stage(last, 1, count, "last")
    both = after(both, last)
    both_new = gather_stage(both, 0, count, "both")
    last = join_rows(last, after(last_new, both))
    last_new = gather_stage(last, 0, count, "last")
    grad_w_down, grad_w_up = call(
        unpack_both_kernel,
        [shape(half, model), shape(model, half)],
        [*both, *after(both_new, last), order],
        [wide(model, half)],
        limit=40,
        smem=(6,),
    )
    last_new = after(last_new, grad_w_down)
    grad_w_query, grad_w_key, grad_w_value, grad_w_out = call(
        unpack_project_kernel,
        [shape(model, width)] * 3 + [shape(width, model)],
        [*last, *last_new, order],
        [wide(model, width)],
        limit=32,
        smem=(6,),
    )
    small = after(small, last)

    flat = small.reshape(-1)
    (
        grad_gain_attn, grad_shift_attn, grad_b_out, grad_gain_ffn, grad_shift_ffn, grad_b_down,
        grad_b_up,
    ) = jnp.split(flat[: 6 * model + half], [model * i for i in range(1, 7)])
    others = small[(6 * model + half) // small.shape[1] :]
    grad_b_query, grad_b_value = others[0, :width], others[1, :width]
    return (
        mixed, grad_tokens, grad_w_query, grad_w_key, grad_w_value, grad_b_query, grad_b_value,
        grad_w_out, grad_b_out, grad_gain_attn, grad_shift_attn, grad_w_up, grad_b_up, grad_w_down,
        grad_b_down, grad_gain_ffn, grad_shift_ffn,
    )


def solution(mesh):
    placed = (
        P(("dp", "tensor"), None),
        P(("dp", "tensor")),
        P(None, "tensor"),
        P(None, "tensor"),
        P(None, "tensor"),
        P("tensor"),
        P("tensor"),
        P("tensor", None),
        P(),
        P(),
        P(),
        P(None, "tensor"),
        P("tensor"),
        P("tensor", None),
        P(),
        P(),
        P(),
        P(("dp", "tensor"), None),
    )
    return jax.shard_map(
        shards,
        mesh=mesh,
        in_specs=placed,
        out_specs=(
            P(("dp", "tensor"), None),
            P(("dp", "tensor"), None),
            P(None, "tensor"),
            P(None, "tensor"),
            P(None, "tensor"),
            P("tensor"),
            P("tensor"),
            P("tensor", None),
            P(),
            P(),
            P(),
            P(None, "tensor"),
            P("tensor"),
            P("tensor", None),
            P(),
            P(),
            P(),
        ),
        check_vma=False,
    )
```

```python
from functools import partial

import jax
import jax.numpy as jnp
from jax import lax
from jax.experimental import pallas as pl
from jax.experimental.pallas import tpu as pltpu
from jax.sharding import PartitionSpec as P

HD = 64
LEN = 1024
EPSILON = 1e-05
MASKED = -1e30
SCALE = HD**-0.5
BLOCKS = 16
PAIR = 2 * HD
MIB = 1 << 20

F32 = jnp.float32
BF16 = jnp.bfloat16


def nn(left, right):
    return lax.dot_general(left, right, (((1,), (0,)), ((), ())), preferred_element_type=F32)


def nt(left, right):
    return lax.dot_general(left, right, (((1,), (1,)), ((), ())), preferred_element_type=F32)


def tn(left, right):
    return lax.dot_general(left, right, (((0,), (0,)), ((), ())), preferred_element_type=F32)


def normalize_parts(hidden):
    average = jnp.mean(hidden, axis=-1, keepdims=True)
    centred = hidden - average
    spread = jnp.mean(centred * centred, axis=-1, keepdims=True)
    inverse = lax.rsqrt(spread + EPSILON)
    return centred * inverse, inverse


def normalize_back(grad_out, normed, inverse, gain):
    scaled = grad_out * gain
    first_mean = jnp.mean(scaled, axis=-1, keepdims=True)
    second_mean = jnp.mean(scaled * normed, axis=-1, keepdims=True)
    return inverse * (scaled - first_mean - normed * second_mean)


def gelu_parts(upper):
    phi = 0.5 + 0.5 * lax.erf(upper * 0.5**0.5)
    bell = jnp.exp(upper * upper * -0.5)
    return upper * phi, phi + upper * bell * 0.3989422804014327


def lasting(us):
    return pl.CostEstimate(flops=int(us * 1.15e9), bytes_accessed=0, transcendentals=0)


def call(kernel, outs, ins, scratch=(), limit=48, smem=(), hbm=(), hbm_outs=(), us=5):
    place = lambda i, far: pl.BlockSpec(memory_space=pl.ANY if i in far else pltpu.VMEM)
    return pl.pallas_call(
        kernel,
        out_shape=outs,
        in_specs=[
            pl.BlockSpec(memory_space=pltpu.SMEM) if i in smem else place(i, hbm)
            for i in range(len(ins))
        ],
        out_specs=[place(i, hbm_outs) for i in range(len(outs))],
        scratch_shapes=list(scratch),
        compiler_params=pltpu.CompilerParams(vmem_limit_bytes=limit * MIB),
        cost_estimate=lasting(us),
    )(*ins)


def shape(*dims, dtype=F32):
    return jax.ShapeDtypeStruct(dims, dtype)


def as_row(ref):
    return ref[...].reshape(1, -1)


def join_segments(refs):
    return jnp.concatenate([as_row(ref).astype(F32) for ref in refs], axis=1)


def as_column(row):
    return jnp.broadcast_to(row, (8, row.shape[1])).T[:, :1]


def pairs(heads):
    return [pl.ds(pair * PAIR, PAIR) for pair in range(heads // 2)]


def split_pair(block):
    owner = lax.broadcasted_iota(jnp.int32, block.shape, 1) // HD
    empty = jnp.zeros_like(block)
    return jnp.concatenate(
        [jnp.where(owner == 0, block, empty), jnp.where(owner == 1, block, empty)], axis=0
    )


def rows_of(order, part, size, split):
    return pl.ds(pl.multiple_of(order[3, part], size) if split > 1 else 0, size)


GRAIN = 128


def by_window(seg, block, body):
    @pl.loop(0, LEN // block)
    def _(j):
        here = seg[:, pl.ds(pl.multiple_of(j * block, block), block)]
        below = (seg[...] < jnp.min(here)).astype(F32)
        within = (seg[...] <= jnp.max(here)).astype(F32)
        first = jnp.sum(below).astype(jnp.int32) // GRAIN
        last = (jnp.sum(within).astype(jnp.int32) + GRAIN - 1) // GRAIN
        sizes = [LEN // 2, 3 * LEN // 4, LEN]
        least = 0
        for size in sizes:
            most = size // GRAIN

            @pl.when(jnp.logical_and(last - first > least, last - first <= most))
            def _(size=size, most=most):
                start = jnp.minimum(first, LEN // GRAIN - most) * GRAIN
                body(j, pl.multiple_of(start, GRAIN), size)

            least = most


def attend_kernel(*refs, split):
    xs, segs, refs = refs[:split], refs[split : 2 * split], refs[2 * split :]
    wq_ref, wk_ref, wv_ref, bq_ref, bv_ref, order = refs[:6]
    q_hbm, k_hbm, v_hbm, *ctx_refs, lse_ref = refs[6 : 10 + split]
    q_ref, k_ref, v_ref, seg, column, vt, ctxt, sems = refs[10 + split :]
    copies = Copies(sems)
    far_rows = pl.ds(pl.program_id(0) * LEN, LEN)
    heads = q_ref.shape[1] // HD
    block = 256
    size = LEN // split
    for i, (x_ref, seg_ref) in enumerate(zip(xs, segs)):
        x, rows = x_ref[...], rows_of(order, i, size, split)
        seg[:, rows] = as_row(seg_ref).astype(F32)
        q_ref[rows, :] = ((nn(x, wq_ref[...]) + as_row(bq_ref)) * SCALE).astype(BF16)
        k_ref[rows, :] = nn(x, wk_ref[...]).astype(BF16)
        value = (nn(x, wv_ref[...]) + as_row(bv_ref)).astype(BF16)
        v_ref[rows, :] = value
        vt[:, rows] = value.T
    for held, far in ((q_ref, q_hbm), (k_ref, k_hbm), (v_ref, v_hbm)):
        copies.store(held, far.at[far_rows, :])
    column[...] = as_column(seg[...])

    def body(j, start, size):
        here = pl.ds(pl.multiple_of(j * block, block), block)
        window = pl.ds(start, size)
        products = [
            nt(k_ref[window, lanes], split_pair(q_ref[here, lanes])) for lanes in pairs(heads)
        ]
        mask = jnp.where(column[window, :] == seg[:, here], 0.0, MASKED)
        weights, tops, totals = [], [], []
        for head in range(heads):
            first = head % 2 * block
            scores = products[head // 2][:, first : first + block] + mask
            tops.append(jnp.max(scores, axis=0, keepdims=True))
            weight = jnp.exp(scores - tops[-1])
            totals.append(jnp.sum(weight, axis=0, keepdims=True))
            weights.append(weight.astype(BF16))
        for head in range(heads):
            at = pl.ds(head * HD, HD)
            ctxt[at, here] = nn(vt[at, window], weights[head]) * (1.0 / totals[head])
            lse_ref[0, pl.ds(head, 1), here] = tops[head] + jnp.log(totals[head])

    by_window(seg, block, body)
    for i, ctx_ref in enumerate(ctx_refs):
        ctx_ref[...] = ctxt[:, rows_of(order, i, size, split)].T.astype(BF16)
    copies.drain()


def attention_forward(xs, segs, w_query, w_key, w_value, b_query, b_value, order):
    split = len(xs)
    size = LEN // split
    rows, model = xs[0].shape[0] // size, xs[0].shape[1]
    width = w_query.shape[1]
    by_part = pl.BlockSpec((size, width), lambda r: (r, 0))
    whole = lambda *dims: pl.BlockSpec(dims, lambda r: (0,) * len(dims))
    us = 13 * rows
    query, key, value, *contexts, lse = pl.pallas_call(
        partial(attend_kernel, split=split),
        grid=(rows,),
        out_shape=[shape(rows * LEN, width, dtype=BF16)] * 3
        + [shape(rows * size, width, dtype=BF16)] * split
        + [shape(rows, 8, LEN)],
        in_specs=[pl.BlockSpec((size, model), lambda r: (r, 0))] * split
        + [pl.BlockSpec((size,), lambda r: (r,))] * split
        + [
            whole(model, width),
            whole(model, width),
            whole(model, width),
            whole(width),
            whole(width),
            pl.BlockSpec(memory_space=pltpu.SMEM),
        ],
        out_specs=[pl.BlockSpec(memory_space=pl.ANY)] * 3
        + [by_part] * split
        + [pl.BlockSpec((1, 8, LEN), lambda r: (r, 0, 0))],
        scratch_shapes=[pltpu.VMEM((LEN, width), BF16)] * 3
        + [
            pltpu.VMEM((1, LEN), F32),
            pltpu.VMEM((LEN, 1), F32),
            pltpu.VMEM((width, LEN), BF16),
            pltpu.VMEM((width, LEN), F32),
            pltpu.SemaphoreType.DMA((3,)),
        ],
        compiler_params=pltpu.CompilerParams(vmem_limit_bytes=62 * MIB),
        cost_estimate=lasting(us),
    )(*xs, *segs, w_query, w_key, w_value, b_query, b_value, order)
    return query, key, value, contexts, lse


def attend_back_kernel(
    q_ref, k_ref, v_ref, lse_ref, order, *refs, first, split
):
    segs, ctx_refs, dctx_refs = (refs[i * split : (i + 1) * split] for i in range(3))
    (
        dq_ref, dk_ref, dv_ref, kt, dqt, dk_sum, dv_sum, inner, dctx_ref, ctx_ref, seg, column
    ) = refs[3 * split :]
    size = LEN // split
    for i in range(split):
        rows = rows_of(order, i, size, split)
        dctx_ref[rows, :] = dctx_refs[i][...]
        ctx_ref[rows, :] = ctx_refs[i][...]
        seg[:, rows] = as_row(segs[i]).astype(F32)
    width = q_ref.shape[1]
    heads = width // HD
    block = 256
    kt[...] = k_ref[...].T
    column[...] = as_column(seg[...])
    picks = lax.broadcasted_iota(jnp.int32, (8, width), 0) == (
        lax.broadcasted_iota(jnp.int32, (8, width), 1) // HD
    )
    product = ctx_ref[...].astype(F32) * dctx_ref[...].astype(F32)
    inner[...] = lax.dot_general(
        picks.astype(F32), product, (((1,), (1,)), ((), ())),
        precision=lax.Precision.HIGHEST, preferred_element_type=F32,
    )
    dk_sum[...] = jnp.zeros_like(dk_sum)
    dv_sum[...] = jnp.zeros_like(dv_sum)

    def body(j, start, size):
        here = pl.ds(pl.multiple_of(j * block, block), block)
        window = pl.ds(start, size)
        allowed = column[window, :] == seg[:, here]
        queries = [split_pair(q_ref[here, lanes]) for lanes in pairs(heads)]
        grads = [split_pair(dctx_ref[here, lanes]) for lanes in pairs(heads)]
        products = [nt(k_ref[window, at], q) for at, q in zip(pairs(heads), queries)]
        slopes = [nt(v_ref[window, at], g) for at, g in zip(pairs(heads), grads)]
        weights, changes = [], []
        for head in range(heads):
            at = slice(head % 2 * block, (head % 2 + 1) * block)
            scores = jnp.where(allowed, products[head // 2][:, at], MASKED)
            weight = jnp.exp(scores - lse_ref[0, first + head : first + head + 1, here])
            change = weight * (slopes[head // 2][:, at] - inner[head : head + 1, here])
            weights.append(weight.astype(BF16))
            changes.append(change.astype(BF16))
        for i, at in enumerate(pairs(heads)):
            both = slice(2 * i, 2 * i + 2)
            dv_sum[window, at] += nn(jnp.concatenate(weights[both], axis=1), grads[i])
            dk_sum[window, at] += nn(jnp.concatenate(changes[both], axis=1), queries[i])
        for head in range(heads):
            at = slice(head * HD, (head + 1) * HD)
            dqt[at, here] = nn(kt[at, window], changes[head]) * SCALE

    by_window(seg, block, body)
    dq_ref[...] = dqt[...].T.astype(BF16)
    dk_ref[...] = dk_sum[...].astype(BF16)
    dv_ref[...] = dv_sum[...].astype(BF16)


def attention_backward(
    place, width, limit, query, key, value, contexts, grads, lse, segs, order
):
    rows, split = query.shape[0] // LEN, len(contexts)
    columns = pl.BlockSpec((LEN, width), lambda r: (r, place))
    part = pl.BlockSpec((LEN // split, width), lambda r: (r, place))
    own = pl.BlockSpec((LEN, width), lambda r: (r, 0))
    us = 6 * width // PAIR * rows
    return pl.pallas_call(
        partial(attend_back_kernel, first=place * width // HD, split=split),
        grid=(rows,),
        out_shape=[shape(rows * LEN, width, dtype=BF16)] * 3,
        in_specs=[columns] * 3
        + [
            pl.BlockSpec((1, 8, LEN), lambda r: (r, 0, 0)),
            pl.BlockSpec(memory_space=pltpu.SMEM),
        ]
        + [pl.BlockSpec((LEN // split,), lambda r: (r,))] * split
        + [part] * (2 * split),
        out_specs=[own] * 3,
        scratch_shapes=[
            pltpu.VMEM((width, LEN), BF16),
            pltpu.VMEM((width, LEN), F32),
            pltpu.VMEM((LEN, width), F32),
            pltpu.VMEM((LEN, width), F32),
            pltpu.VMEM((8, LEN), F32),
            pltpu.VMEM((LEN, width), BF16),
            pltpu.VMEM((LEN, width), BF16),
            pltpu.VMEM((1, LEN), F32),
            pltpu.VMEM((LEN, 1), F32),
        ],
        compiler_params=pltpu.CompilerParams(vmem_limit_bytes=limit * MIB),
        cost_estimate=lasting(us),
    )(query, key, value, lse, order, *segs, *contexts, *grads)


def rearrange(order, source, target):
    third = source.shape[0] // 3
    size = third // BLOCKS
    for p in range(3):
        for place in range(BLOCKS):
            rows = pl.ds(pl.multiple_of(p * third + order[p, place] * size, 16), size)
            target[pl.ds(p * third + place * size, size), :] = source[rows, :]


class Copies:
    def __init__(self, sems):
        self.sems, self.used, self.open = sems, 0, []

    def start(self, source, target):
        copy = pltpu.make_async_copy(source, target, self.sems.at[self.used])
        self.used += 1
        copy.start()
        return copy

    def store(self, source, target):
        self.open.append(self.start(source, target))

    def drain(self):
        for copy in self.open:
            copy.wait()


def as_lines(row, cols):
    return jnp.concatenate(
        [row[:, i : i + cols] for i in range(0, row.shape[1], cols)], axis=0
    )


def split_small(values):
    high = values.astype(BF16)
    return jnp.concatenate([high, (values - high.astype(F32)).astype(BF16)], axis=0)


def layer_kernel(
    x_ref, ctx_a, ctx_b, wo_a, wo_b, b_out, gain_one, shift_one, b_down, gain_two, shift_two,
    bu_a, bu_b, order, wu_a, wu_b, wd_a, wd_b, cot_hbm,
    sums_ref, gctx_a, gctx_b, out_a, out_b, mixed_hbm, one_hbm, down_a, down_b, up_a, up_b,
    wu, wd, cot, mixed, after_buf, normed_buf, inverse_buf, slope, grad_buf, low_buf, act,
    flipped, moved, parts, total, sems,
):
    rows, model = x_ref.shape
    half = wu_a.shape[1]
    chunk = 768
    copies = Copies(sems)
    ups, downs = [], []
    for side, up in enumerate((wu_a, wu_b)):
        for start in range(0, half, chunk):
            to = pl.ds(side * half + start, chunk)
            ups.append(copies.start(up.at[:, pl.ds(start, chunk)], wu.at[:, to]))
    for side, down in enumerate((wd_a, wd_b)):
        downs.append(copies.start(down, wd.at[pl.ds(side * half, half), :]))
    cot_copy = copies.start(cot_hbm, cot)
    b_out, gain_one, shift_one, b_down, gain_two, shift_two = map(
        as_row, (b_out, gain_one, shift_one, b_down, gain_two, shift_two)
    )
    biases = [as_row(bu_a), as_row(bu_b)]

    hidden = nn(ctx_a[...], wo_a[...]) + nn(ctx_b[...], wo_b[...])
    normed, inverse = normalize_parts(x_ref[...].astype(F32) + hidden + b_out)
    normed_buf[...] = normed
    inverse_buf[...] = inverse
    after_buf[...] = (normed * gain_one + shift_one).astype(BF16)

    def raise_up(i):
        ups[i].wait()
        here = pl.ds(i * chunk, chunk)
        start = i * chunk % half
        bias = biases[i * chunk // half][:, start : start + chunk]
        return nn(after_buf[...], wu[:, here]) + bias

    count = 2 * half // chunk
    for i in range(count):
        upper = raise_up(i)
        here = pl.ds(i * chunk, chunk)
        active, steep = gelu_parts(upper)
        act[:, here] = active.astype(BF16)
        slope[:, here] = steep.astype(BF16)
    for copy in downs:
        copy.wait()
    total[...] = nn(act[...], wd[...])
    cot_copy.wait()

    after = normed_buf[...] * gain_one + shift_one
    normed, inverse = normalize_parts(after + total[...] + b_down)
    mixed[...] = (normed * gain_two + shift_two).astype(BF16)
    copies.store(mixed, mixed_hbm)
    outer = cot[...].astype(F32)
    grad = normalize_back(outer, normed, inverse, gain_two)
    grad_buf[...] = grad
    low_buf[...] = grad.astype(BF16)
    add_up = lambda values: jnp.sum(values, axis=0, keepdims=True)
    sums_two = [add_up(outer * normed), add_up(outer), add_up(grad)]

    flipped[...] = grad_buf[...].T.astype(BF16)
    rearrange(order, flipped, moved)
    for side, out in ((1, down_b), (0, down_a)):
        parts[side] = nn(moved[...], act[:, pl.ds(side * half, half)]).astype(BF16)
        copies.store(parts.at[side], out)
    flipped[...] = after_buf[...].T
    rearrange(order, flipped, moved)
    sums_up = [None, None]
    for side, out in ((1, up_b), (0, up_a)):
        here = pl.ds(side * half, half)
        pulled = nt(low_buf[...], wd[here, :])
        slope[:, here] = (pulled * slope[:, here].astype(F32)).astype(BF16)
        sums_up[side] = add_up(slope[:, here].astype(F32))
        parts[2 + side] = nn(moved[...], slope[:, here]).astype(BF16)
        copies.store(parts.at[2 + side], out)
    total[...] = nt(slope[...], wu[...])

    after = grad_buf[...] + total[...]
    normed = normed_buf[...]
    grad = normalize_back(after, normed, inverse_buf[...], gain_one)
    grad_buf[...] = grad
    copies.store(grad_buf, one_hbm)
    low_buf[...] = grad.astype(BF16)
    gctx_b[...] = nt(low_buf[...], wo_b[...]).astype(BF16)
    gctx_a[...] = nt(low_buf[...], wo_a[...]).astype(BF16)
    flipped[...] = grad_buf[...].T.astype(BF16)
    rearrange(order, flipped, moved)
    out_b[pl.ds(0, model), :] = nn(moved[...], ctx_b[...]).astype(BF16)
    out_a[...] = nn(moved[...], ctx_a[...]).astype(BF16)

    cols = ctx_a.shape[1] // 3
    sums = [add_up(after * normed), add_up(after), add_up(grad), *sums_two]
    shared = as_lines(jnp.concatenate(sums, axis=1), cols)
    own, other = (as_lines(part, cols) for part in sums_up)
    sums_ref[...] = jnp.concatenate([shared, own], axis=0)
    rider = split_small(jnp.concatenate([shared, other], axis=0))
    lines = rider.shape[0] // 3
    for i in range(3):
        out_b[pl.ds(model, lines), pl.ds(i * cols, cols)] = rider[i * lines : (i + 1) * lines]
    copies.drain()


SMALL = 16


def project_kernel(*refs):
    x_a, x_b, out_a, out_b, sums_ref, order = refs[:6]
    grads, outs = refs[6:12], refs[12:]
    keeps, sends, (small, joint, flipped, moved) = outs[:3], outs[3:6], outs[6:]
    width = joint.shape[1] // 3
    cols = width // 3
    here, model = x_a.shape
    half = keeps[0].shape[0]
    for i, x_ref in enumerate((x_a, x_b)):
        flipped[:, pl.ds(pl.multiple_of(order[3, i], here), here)] = x_ref[...].T
    for i, grad in enumerate(grads):
        start = i % 3 * width + i // 3 * (width - PAIR)
        joint[:, pl.ds(start, grad.shape[1])] = grad[...]
    rearrange(order, flipped, moved)
    product = nn(moved[...], joint[...]).astype(BF16)
    other = (out_a[...].astype(F32) + out_b[pl.ds(0, model), :].astype(F32)).astype(BF16)
    for p in range(3):
        for i, out in enumerate((keeps[p], sends[p])):
            rows = slice((2 * p + i) * half, (2 * p + i + 1) * half)
            out[pl.ds(0, half), pl.ds(0, 3 * width)] = product[rows]
            out[pl.ds(0, half), pl.ds(3 * width, width)] = other[rows]
    sums = jnp.sum(joint[...].astype(F32), axis=0, keepdims=True)
    lines = out_b.shape[0] - model
    rider = [out_b[pl.ds(model, lines), pl.ds(i * cols, cols)] for i in range(3)]
    rider = jnp.concatenate(rider, axis=0).astype(F32)
    count = sums_ref.shape[0]
    shared = sums_ref[...] + (rider[:count] + rider[count:])
    per = small.shape[1] // cols
    small[...] = jnp.zeros_like(small)
    for i in range(count):
        small[pl.ds(i // per, 1), pl.ds(i % per * cols, cols)] = shared[i : i + 1]
    rows = count // per
    small[pl.ds(rows, 1), pl.ds(0, width)] = sums[:, :width]
    small[pl.ds(rows + 1, 1), pl.ds(0, width)] = sums[:, 2 * width :]
    sends[0][pl.ds(half, SMALL), :] = jnp.zeros((SMALL, sends[0].shape[1]), BF16)
    high = split_small(small[...])
    for i in range(2):
        sends[0][pl.ds(half, SMALL), pl.ds(i * small.shape[1], small.shape[1])] = high[
            i * SMALL : (i + 1) * SMALL
        ]


def tokens_kernel(joint, w_query, w_key, w_value, grad_one, order, part_ref, own_ref):
    rows, width = own_ref.shape[0], w_query.shape[1]
    for side, out_ref in ((1, part_ref), (0, own_ref)):
        total = grad_one[...] if side == 0 else 0.0
        at = pl.ds(pl.multiple_of(order[3, side], rows), rows)
        for i, weight in enumerate((w_query, w_key, w_value)):
            part = joint[at, pl.ds(i * width, width)]
            total = total + nt(part, weight[...])
        out_ref[...] = total.astype(out_ref.dtype)


def unpack(order, lows, highs, put):
    third = 2 * lows[0].shape[0]
    size = third // BLOCKS
    for p, halves_of_part in enumerate(zip(lows, highs)):
        for place in range(BLOCKS):
            rows = pl.ds(pl.multiple_of(p * third + order[p, place] * size, 8), size)
            side, at = divmod(place, BLOCKS // 2)
            put(rows, halves_of_part[side][pl.ds(at * size, size), :].astype(F32))


def unpack_both_kernel(*refs):
    lows, highs, (order, down_ref, up_ref, natural) = refs[:3], refs[3:6], refs[6:]
    half = up_ref.shape[1]

    def put(rows, values):
        natural[rows, :] = values[:, :half]
        up_ref[rows, :] = values[:, half:]

    unpack(order, lows, highs, put)
    step = 512
    for start in range(0, half, step):
        here = pl.ds(start, step)
        down_ref[here, :] = natural[:, here].T


def unpack_project_kernel(*refs):
    lows, highs, refs = refs[:3], refs[3:6], refs[6:]
    order, q_ref, k_ref, v_ref, out_ref, natural = refs
    width = q_ref.shape[1]

    def put(rows, values):
        for i, ref in enumerate((q_ref, k_ref, v_ref, natural)):
            ref[rows, :] = values[:, i * width : (i + 1) * width]

    unpack(order, lows, highs, put)
    out_ref[...] = natural[...].T


def swap(value, bit, count, name="swap"):
    with jax.named_scope(name):
        return lax.ppermute(value, "dp", [(i, i ^ bit) for i in range(count)])


def across(value):
    return lax.ppermute(value, "tensor", [(0, 1), (1, 0)])


def add(left, right):
    return (left.astype(F32) + right.astype(F32)).astype(BF16)


STAGES = ((1, 2, 4, 8), (2, 4, 1, 8), (4, 1, 2, 8))


def block_order(base, here):
    mine = lax.rem(lax.axis_index("dp"), BLOCKS // 2)
    rows = []
    for bits in STAGES:
        rows.append(
            [
                sum(bit for i, bit in enumerate(bits) if place >> (len(bits) - 1 - i) & 1)
                for place in range(BLOCKS)
            ]
        )
    rows = jnp.bitwise_xor(jnp.array(rows, jnp.int32), mine.astype(jnp.int32))
    bases = jnp.stack([base, here - base]).astype(jnp.int32)
    return jnp.concatenate([rows, jnp.pad(bases, (0, BLOCKS - 2))[None]], axis=0)


def halves(own, other):
    half = own.shape[0] // 6
    cut = lambda at: add(own[at * half : (at + 1) * half], other[at * half : (at + 1) * half])
    return [cut(2 * p) for p in range(3)], [cut(2 * p + 1) for p in range(3)]


def send_stage(sends, step, count, name):
    return [
        swap(sends[p], STAGES[p][step], count, f"{name}_send{step}_{p}") for p in range(3)
    ]


def next_halves(keeps, gots):
    half = keeps[0].shape[0] // 2
    cut = lambda side: [
        add(keeps[p][side * half : (side + 1) * half], gots[p][side * half : (side + 1) * half])
        for p in range(3)
    ]
    return cut(0), cut(1)


def with_rider(rows, small):
    high = split_small(small)
    rider = jnp.concatenate([high[:SMALL], high[SMALL:]], axis=1)
    rider = jnp.pad(rider, ((0, 0), (0, rows.shape[1] - rider.shape[1])))
    return jnp.concatenate([rows, rider], axis=0)


def take_small(got, rows, small):
    rider, width = got[rows:].astype(F32), small.shape[1]
    return got[:rows], small + (rider[:, :width] + rider[:, width : 2 * width])


def halves_and_small(keeps, gots, small):
    first, small = take_small(gots[0], keeps[0].shape[0], small)
    keeps, sends = next_halves(keeps, [first, *gots[1:]])
    return keeps, [with_rider(sends[0], small), *sends[1:]], small


def gather_stage(values, step, count, name):
    return [
        swap(values[p], STAGES[p][step], count, f"{name}_gather{step}_{p}") for p in range(3)
    ]


def after(values, *earlier):
    return lax.optimization_barrier((values, *earlier))[0]


def shards(
    tokens, segment_ids, w_query, w_key, w_value, b_query, b_value, w_out, b_out, gain_attn,
    shift_attn, w_up, b_up, w_down, b_down, gain_ffn, shift_ffn, cotangent,
):
    count = lax.axis_size("dp")
    here, model = tokens.shape
    width, half = w_query.shape[1], w_up.shape[1]
    row = lambda vector: vector.reshape(1, -1)

    tokens_b = across(tokens)
    segments_b, bu_b = across(segment_ids), across(b_up)
    arrived = (tokens_b, segments_b, bu_b)
    wo_b, wu_b, wd_b = map(across, after((w_out, w_up, w_down), arrived))
    one_row = here < LEN
    order = block_order(lax.axis_index("tensor") * here if one_row else 0 * count, here)
    lay = lambda own, other: (
        [own, other] if one_row else [jnp.concatenate([own, other], axis=0)]
    )
    segs = lay(segment_ids, segments_b)
    query, key, value, contexts, lse = attention_forward(
        lay(tokens, tokens_b), segs, w_query, w_key, w_value, b_query, b_value, order
    )
    if one_row:
        ctx_a, ctx_b = contexts
    else:
        ctx_a, ctx_b = contexts[0][:here], contexts[0][here:]
    ctx_b = across(ctx_b)

    low = lambda *dims: shape(*dims, dtype=BF16)
    held = lambda *dims: pltpu.VMEM(dims, BF16)
    wide = lambda *dims: pltpu.VMEM(dims, F32)
    lines = (6 * model + half) // (width // 3)
    size = min(here, LEN // 2)

    def layer(at):
        cut = lambda value: value[at : at + size]
        return call(
            layer_kernel,
            [
                shape(lines, width // 3), low(size, width), low(size, width), low(model, width),
                low(model + 2 * lines // 3, width), low(size, model), shape(size, model),
            ] + [low(model, half)] * 4,
            [
                cut(tokens), cut(ctx_a), cut(ctx_b), w_out, wo_b, b_out, gain_attn, shift_attn,
                b_down, gain_ffn, shift_ffn, b_up, bu_b, order, w_up, wu_b, w_down, wd_b,
                cut(cotangent),
            ],
            [
                held(model, 2 * half), held(2 * half, model), held(size, model), held(size, model),
                held(size, model), wide(size, model), wide(size, 1), held(size, 2 * half),
                wide(size, model), held(size, model), held(size, 2 * half), held(model, size),
                held(model, size), held(4, model, half), wide(size, model),
                pltpu.SemaphoreType.DMA((20,)),
            ],
            limit=62,
            smem=(13,),
            hbm=(14, 15, 16, 17, 18),
            hbm_outs=range(5, 11),
            us=32,
        )

    blocks = [layer(at) for at in range(0, here, size)]
    if len(blocks) == 1:
        small_sums, gctx_a, gctx_b, out_a, out_b, mixed, grad_one, *weights = blocks[0]
    else:
        small_sums, gctx_a, gctx_b, out_a, out_b, mixed, grad_one, *weights = (
            jnp.concatenate(each, axis=0)
            if i in (1, 2, 5, 6)
            else sum(part.astype(F32) for part in each).astype(each[0].dtype)
            for i, each in enumerate(zip(*blocks))
        )
    down_a, down_b, up_a, up_b = weights
    grad_contexts = lay(gctx_a, across(gctx_b))
    down_b, up_b, out_b = after((down_b, up_b, out_b), grad_contexts)
    down_got, up_got, out_got = across(down_b), across(up_b), across(out_b)

    back = lambda place, columns, limit, earlier: attention_backward(
        place, columns, limit, query, key, value, contexts, after(grad_contexts, earlier), lse,
        segs, order,
    )
    grads = back(width // PAIR - 1, PAIR, 62, grad_contexts)
    down_got, up_got = after((down_got, up_got), grads)
    down_keep, down_send = halves(down_a, down_got)
    up_keep, up_send = halves(up_a, up_got)
    join = lambda one, two: [jnp.concatenate(pair, axis=1) for pair in zip(one, two)]
    both_keep, both_send = join(down_keep, up_keep), join(down_send, up_send)
    both_new = send_stage(both_send, 0, count, "both")

    grads = [*back(0, width - PAIR, 30, (grads, both_send)), *grads]
    sixth = low(model // 6, 4 * width)
    *last, small, joint = call(
        project_kernel,
        [sixth] * 3
        + [low(model // 6 + SMALL, 4 * width), sixth, sixth]
        + [shape(SMALL, half // 3), low(2 * here, 3 * width)],
        [
            tokens, tokens_b, out_a, out_got, small_sums, order, *grads,
        ],
        [held(model, 2 * here), held(model, 2 * here)],
        smem=(5,),
        us=7,
    )
    last_keep, last_send = last[:3], last[3:]
    both_keep, both_send = next_halves(both_keep, after(both_new, last))
    both_new = send_stage(both_send, 1, count, "both")
    last_send = after(last_send, both_send)
    last_new = send_stage(last_send, 0, count, "last")
    token_part, token_own = call(
        tokens_kernel,
        [low(here, model), shape(here, model)],
        [after(joint, last_send), w_query, w_key, w_value, grad_one, order],
        smem=(5,),
        us=5,
    )
    token_got = across(token_part)

    join_rows = lambda one, two: [jnp.concatenate(pair, axis=0) for pair in zip(one, two)]
    meet = lambda keeps, gots: jnp.concatenate([add(k, g) for k, g in zip(keeps, gots)], axis=0)
    apart = lambda value: [
        value[i * value.shape[0] // 3 : (i + 1) * value.shape[0] // 3] for i in range(3)
    ]
    extras = [BLOCKS // 2 << i for i in range((count // (BLOCKS // 2)).bit_length() - 1)]
    both_keep, both_send = next_halves(both_keep, after(both_new, token_own))
    both_new = send_stage(both_send, 2, count, "both")
    last_new = after(last_new, both_send)
    last_keep, last_send, small = halves_and_small(last_keep, last_new, small)
    last_new = send_stage(last_send, 1, count, "last")
    both_new = after(both_new, last_send)
    both_value = meet(both_keep[:2], both_new[:2])
    both_got = swap(both_value, extras[0], count, "both_exchange")
    third_value = meet(both_keep[2:], after(both_new[2:], both_value))

    last_new = after(last_new, both_value)
    last_keep, last_send, small = halves_and_small(last_keep, last_new, small)
    last_new = send_stage(last_send, 2, count, "last")
    third_value = after(third_value, last_send)
    third_got = swap(third_value, extras[0], count, "third_exchange")
    grad_tokens = token_own + after(token_got, last_send).astype(F32)
    first, small = take_small(last_new[0], last_keep[0].shape[0], small)
    last_value = meet(last_keep, [first, *last_new[1:]])
    rider = with_rider(last_value, small)
    last_got = swap(rider, extras[0], count, "last_exchange")

    both_value = jnp.concatenate([both_value, third_value], axis=0)
    both_got = jnp.concatenate(after([both_got, third_got], rider), axis=0)
    both_value = add(both_value, both_got)
    for extra in extras[1:]:
        both_value = add(both_value, swap(both_value, extra, count))
    both = apart(both_value)
    both = join_rows(both, gather_stage(both, 2, count, "both"))
    both_new = gather_stage(both, 1, count, "both")

    last_got, small = take_small(after(last_got, both), last_value.shape[0], small)
    last_value = add(last_value, last_got)
    for extra in extras[1:]:
        got = swap(with_rider(last_value, small), extra, count)
        got, small = take_small(got, last_value.shape[0], small)
        last_value = add(last_value, got)
    last = apart(last_value)
    last_new = gather_stage(last, 2, count, "last")
    both = join_rows(both, after(both_new, last))
    last = join_rows(last, after(last_new, both))
    last_new = gather_stage(last, 1, count, "last")
    both = after(both, last)
    both_new = gather_stage(both, 0, count, "both")
    last = join_rows(last, after(last_new, both))
    last_new = gather_stage(last, 0, count, "last")
    grad_w_down, grad_w_up = call(
        unpack_both_kernel,
        [shape(half, model), shape(model, half)],
        [*both, *after(both_new, last), order],
        [wide(model, half)],
        limit=40,
        smem=(6,),
    )
    last_new = after(last_new, grad_w_down)
    grad_w_query, grad_w_key, grad_w_value, grad_w_out = call(
        unpack_project_kernel,
        [shape(model, width)] * 3 + [shape(width, model)],
        [*last, *last_new, order],
        [wide(model, width)],
        limit=32,
        smem=(6,),
    )
    small = after(small, last)

    flat = small.reshape(-1)
    (
        grad_gain_attn, grad_shift_attn, grad_b_out, grad_gain_ffn, grad_shift_ffn, grad_b_down,
        grad_b_up,
    ) = jnp.split(flat[: 6 * model + half], [model * i for i in range(1, 7)])
    others = small[(6 * model + half) // small.shape[1] :]
    grad_b_query, grad_b_value = others[0, :width], others[1, :width]
    return (
        mixed, grad_tokens, grad_w_query, grad_w_key, grad_w_value, grad_b_query, grad_b_value,
        grad_w_out, grad_b_out, grad_gain_attn, grad_shift_attn, grad_w_up, grad_b_up, grad_w_down,
        grad_b_down, grad_gain_ffn, grad_shift_ffn,
    )


def solution(mesh):
    placed = (
        P(("dp", "tensor"), None),
        P(("dp", "tensor")),
        P(None, "tensor"),
        P(None, "tensor"),
        P(None, "tensor"),
        P("tensor"),
        P("tensor"),
        P("tensor", None),
        P(),
        P(),
        P(),
        P(None, "tensor"),
        P("tensor"),
        P("tensor", None),
        P(),
        P(),
        P(),
        P(("dp", "tensor"), None),
    )
    return jax.shard_map(
        shards,
        mesh=mesh,
        in_specs=placed,
        out_specs=(
            P(("dp", "tensor"), None),
            P(("dp", "tensor"), None),
            P(None, "tensor"),
            P(None, "tensor"),
            P(None, "tensor"),
            P("tensor"),
            P("tensor"),
            P("tensor", None),
            P(),
            P(),
            P(),
            P(None, "tensor"),
            P("tensor"),
            P("tensor", None),
            P(),
            P(),
            P(),
        ),
        check_vma=False,
    )
```
